32 devices in a mesh: group: 4 (over y, x), member: 8 (over z, core).
Axes of the slice: x: 2, y: 2, z: 4, core: 2. Of those that a mesh axis runs over, the one named last changes fastest.
Arguments:
- tokens: bfloat16 [4096, 2048], P(('group', 'member')), may hold values from -6 to 6
- cotangent: bfloat16 [4096, 2048], P(('group', 'member')), may hold values from -6 to 6
- w_gate: bfloat16 [2048, 512], P('member'), may hold values from -0.125 to 0.125
- w_up: bfloat16 [2048, 512], P('member'), may hold values from -0.125 to 0.125
- w_down: bfloat16 [2048, 512], P('member'), may hold values from -0.125 to 0.125
- basis: float32 [2048, 256], P('member'), may hold values from -0.088388348 to 0.088388348
- first_moment: float32 [3, 256, 512], P(None, 'member'), may hold values from -3 to 3
- second_moment: float32 [3, 256, 512], P(None, 'member'), may hold values from 0.1 to 2
Outputs:
- input_grad: bfloat16 [4096, 2048], P(('group', 'member'))
- new_first: float32 [3, 256, 512], P(None, 'member')
- new_second: float32 [3, 256, 512], P(None, 'member')
- updates: float32 [3, 2048, 512], P(None, 'member')
The draws below stay inside these ranges and needn't reach their ends.
All inputs are finite; a program needn't handle non-finite values.
Results may differ from the reference program's by a relative error of at most 0.008.
Values may be sent and summed in bfloat16 or wider, within the bound.
No kernel may reach another device: no remote copies, remote signals or barrier semaphores. Data moves between devices by JAX's collectives and lax.ppermute only.
A program may use at most 64 MiB of HBM per device.

```python
import math
import jax
import jax.numpy as jnp
from jax import lax

D = 2048
FF = 512
RANK = 256
TOK_DEV = 128
TOKENS = 4096
N_GROUP = 4
N_MEMBER = 8


def draw_basis(key, part):
    noise_key = jax.random.fold_in(key, 11)
    position = jnp.arange(RANK, dtype=jnp.float32) / max(RANK - 1, 1)
    values = jax.random.normal(noise_key, (D, RANK), jnp.float32)
    values = jnp.clip(values, -6.0, 6.0)
    column = 1.0 + 2.0 * position
    edge = 4.0 / jnp.sqrt(jnp.float32(D))
    scaled = values * column[None, :] / jnp.sqrt(jnp.float32(D))
    return jnp.clip(scaled, -edge, edge)


def block_scale(rng, extent, shards, smallest, high):
    def one(dim, parts):
        heights = jax.random.uniform(jax.random.fold_in(jax.random.fold_in(rng, 6), dim), (parts,), jnp.float32, smallest / len(shards), high / len(shards))
        return jnp.repeat(jnp.exp(heights), extent[dim] // parts).reshape((-1,) + (1,) * (len(extent) - dim - 1))

    gain = one(*shards[0])
    for cut in shards[1:]:
        gain = gain * one(*cut)
    return gain


def gaussian(rng, extent, spread, most, split=(), kind=jnp.bfloat16):
    array = jax.random.normal(rng, extent, jnp.float32) * spread
    if len(split) > 0:
        array = block_scale(rng, extent, split, -0.22, 0.18) * array
    return jnp.clip(array, min=-most, max=most).astype(kind)


def setup_inputs(seed: int = 0) -> dict:
    seeds = jax.random.split(jax.random.key(seed), 9)
    tokens = gaussian(seeds[0], (TOKENS, D), 1.0, 6.0, ((0, 32),))
    cotangent = gaussian(seeds[1], (TOKENS, D), 1.0, 6.0, ((0, 32),))
    w_gate = gaussian(seeds[2], (D, FF), D ** -0.5, 0.125, ((0, 8),))
    w_up = gaussian(seeds[3], (D, FF), D ** -0.5, 0.125, ((0, 8),))
    w_down = gaussian(seeds[4], (D, FF), D ** -0.5, 0.125, ((0, 8),))
    basis = draw_basis(jax.random.fold_in(seeds[8], 71), 0)
    first_moment = gaussian(seeds[6], (3, RANK, FF), 0.5, 3.0, ((1, 8),), jnp.float32)
    second_moment = jnp.clip(jnp.exp(math.log(2.0) - 2.9957323 * jax.random.uniform(seeds[7], (3, RANK, FF), jnp.float32) ** block_scale(seeds[7], (3, RANK, FF), ((1, 8),), -0.2, 0.2)), 0.1, 2.0)
    return {"tokens": tokens, "cotangent": cotangent, "w_gate": w_gate, "w_up": w_up, "w_down": w_down, "basis": basis, "first_moment": first_moment, "second_moment": second_moment}


def reference(tokens, cotangent, w_gate, w_up, w_down, basis, first_moment, second_moment):
    count = N_GROUP * N_MEMBER
    x_blocks = tokens.reshape(count, TOK_DEV, D)
    y_blocks = cotangent.reshape(count, TOK_DEV, D)

    def one_block(carry, pair):
        x_rows, y_rows = pair
        gate = jnp.dot(x_rows, w_gate, preferred_element_type=jnp.float32)
        up = jnp.dot(x_rows, w_up, preferred_element_type=jnp.float32)
        sig = jax.nn.sigmoid(gate)
        silu = gate * sig
        hidden = (silu * up).astype(jnp.bfloat16)
        dhid = jnp.dot(y_rows, w_down, preferred_element_type=jnp.float32)
        dgate = (dhid * up * sig * (1.0 + gate * (1.0 - sig))).astype(jnp.bfloat16)
        dup = (dhid * silu).astype(jnp.bfloat16)
        dx = lax.dot_general(dgate, w_gate, (((1,), (1,)), ((), ())), preferred_element_type=jnp.float32)
        dx = dx + lax.dot_general(dup, w_up, (((1,), (1,)), ((), ())), preferred_element_type=jnp.float32)
        grad_gate = lax.dot_general(x_rows, dgate, (((0,), (0,)), ((), ())), preferred_element_type=jnp.float32)
        grad_up = lax.dot_general(x_rows, dup, (((0,), (0,)), ((), ())), preferred_element_type=jnp.float32)
        grad_down = lax.dot_general(y_rows, hidden, (((0,), (0,)), ((), ())), preferred_element_type=jnp.float32)
        carry = carry + jnp.stack([grad_gate, grad_up, grad_down])
        return (carry, dx.astype(jnp.bfloat16))
    start = jnp.zeros((3, D, FF), jnp.float32)
    grads, dx_blocks = lax.scan(one_block, start, (x_blocks, y_blocks))
    input_grad = dx_blocks.reshape(TOKENS, D)
    lowrank = jnp.einsum('dr,kdf->krf', basis, grads, precision=lax.Precision.HIGHEST)
    limit = math.sqrt(3.0 * RANK * FF)
    factor = jnp.minimum(1.0, limit / jnp.sqrt(jnp.sum(lowrank * lowrank) + 1e-06))
    grad_low = factor * lowrank
    new_first = 0.5 * first_moment + 0.5 * grad_low
    new_second = 0.9 * second_moment + 0.1 * grad_low * grad_low
    step = (new_first / (jnp.sqrt(new_second) + 1e-08)).astype(jnp.bfloat16)
    updates = jnp.einsum('dr,krf->kdf', basis, step.astype(jnp.float32), precision=lax.Precision.HIGHEST)
    return (input_grad, new_first, new_second, updates)
```

```python
import functools
import math

import jax
import jax.numpy as jnp
from jax import lax
from jax.experimental import pallas as pl
from jax.experimental.pallas import tpu as pltpu
from jax.sharding import PartitionSpec as P

BF = jnp.bfloat16
F32 = jnp.float32
ROWS = (((0,), (0,)), ((), ()))
COLS = (((1,), (1,)), ((), ()))


def dot(left, right, dims=(((1,), (0,)), ((), ()))):
    return lax.dot_general(left, right, dims, preferred_element_type=F32)


def whole(count):
    return [pl.BlockSpec(memory_space=pltpu.VMEM)] * count


def call(body, outs, scratch, flops, *operands):
    moved = sum(o.size * o.dtype.itemsize for o in operands)
    moved += sum(math.prod(s) * jnp.dtype(d).itemsize for s, d in outs)
    return pl.pallas_call(
        body,
        out_shape=[jax.ShapeDtypeStruct(s, d) for s, d in outs],
        in_specs=whole(len(operands)),
        out_specs=whole(len(outs)),
        scratch_shapes=scratch,
        compiler_params=pltpu.CompilerParams(vmem_limit_bytes=40 * 1024 * 1024),
        cost_estimate=pl.CostEstimate(
            flops=flops, bytes_accessed=moved, transcendentals=0
        ),
    )(*operands)


def places():
    group, member = lax.axis_index("group"), lax.axis_index("member")
    return group % 2, (group // 2) % 2, member // 2, member % 2, member


def sources(count):
    _, high, _, _, member = places()
    order = [member, member ^ 1]
    for k in range(1, count // 2):
        near = member ^ (2 * k) ^ high
        order += [near, near ^ 1]
    return order


def joined(refs):
    return jnp.concatenate([ref[...] for ref in refs], axis=0)


def place_blocks(members, blocks, full):
    depth = blocks[0].shape[0]
    for src, block in zip(sources(members), blocks):
        full[pl.ds(pl.multiple_of(src * depth, depth), depth), :] = block[...]


def first_kernel(members, *refs):
    toks, cots, blocks = refs[:4], refs[4:8], refs[8 : 8 + members]
    dhid_ref, proj_ref, full = refs[8 + members :]
    unit = dhid_ref.shape[1]
    half = proj_ref.shape[1] // 2
    place_blocks(members, blocks, full)
    from_cot = dot(joined(cots), full[...])
    dhid_ref[...] = from_cot[:, :unit]
    proj_ref[:, :half] = dot(joined(toks), full[:, unit:]).astype(BF)
    proj_ref[:, half:] = from_cot[:, unit:].astype(BF)


def second_kernel(members, *refs):
    chips = members // 2
    tok_refs, blocks = refs[:4], refs[4 : 4 + members]
    dhid_ref, mine_ref, other_ref = refs[4 + members : 7 + members]
    dgu_ref, *low_refs, low, full = refs[7 + members :]
    unit = dhid_ref.shape[1]
    half = mine_ref.shape[1] // 2
    _, _, chip, core, _ = places()
    place_blocks(members, blocks, full)
    total = dot(joined(tok_refs), full[...])
    gate, up, dhid = total[:, :unit], total[:, unit:], dhid_ref[...]
    sig = 1.0 / (1.0 + jnp.exp(-gate))
    silu = gate * sig
    hidden = (silu * up).astype(BF)
    dgate = (dhid * up * sig * (1.0 + gate * (1.0 - sig))).astype(BF)
    dup = (dhid * silu).astype(BF)
    dgu = jnp.concatenate([dgate, dup], axis=1)
    dgu_ref[...] = dgu
    toks = mine_ref.shape[0] // 4
    other = jnp.concatenate(
        [other_ref[i * toks : (i + 1) * toks, :] for i in (1, 0, 3, 2)], axis=0
    )
    for away, proj in enumerate((mine_ref[...], other)):
        rows = pl.ds(away * half, half)
        tok_low = dot(proj[:, :half], dgu, ROWS)
        low[0, rows, :] = tok_low[:, :unit]
        low[1, rows, :] = tok_low[:, unit:]
        low[2, rows, :] = dot(proj[:, half:], hidden, ROWS)
    height = low_refs[0].shape[1]
    for k, ref in enumerate(low_refs):
        row = (chip ^ k) * height
        row = (row // half ^ core) * half + row % half
        rows = pl.ds(pl.multiple_of(row, height), height)
        for i in range(ref.shape[0]):
            ref[i] = low[i, rows, :].astype(ref.dtype)


def grad_kernel(members, *refs):
    dgu_ref, blocks, full = refs[0], refs[1 : 1 + members], refs[-1]
    keep_0, keep_1, send_0, send_1 = refs[1 + members : 5 + members]
    toks = keep_0.shape[0]
    place_blocks(members, blocks, full)
    for i, ref in enumerate((keep_0, send_0, keep_1, send_1)):
        part = dot(dgu_ref[i * toks : (i + 1) * toks, :], full[...], COLS)
        ref[...] = part.astype(ref.dtype)


def last_kernel(chips, limit, *refs):
    lows, (core_low, moms, core_moms) = refs[:2], refs[2:5]
    basis_ref, first_ref, second_ref, new_first_ref, new_second_ref, upd_ref = refs[5:11]
    full, stepped = refs[11:]
    side, _, chip, core, member = places()
    height, unit = lows[0].shape[2:]
    pieces = []
    squares = None
    for dc in range(2):
        for dx in range(2):
            column = ((side ^ dx) * 2 + (core ^ dc)) * unit
            columns = pl.ds(pl.multiple_of(column, unit), unit)
            for k in range(chips):
                low = (core_low[dx, k] if dc else lows[dx][k]).astype(F32)
                square = jnp.sum(low * low, axis=(0, 1), keepdims=True)
                squares = square if squares is None else squares + square
                pieces.append((dc, dx, k, columns, low))
                rows = pl.ds(pl.multiple_of((chip ^ k) * height, height), height)
                full[:, rows, columns] = low
    total = jnp.sum(squares, axis=2, keepdims=True)
    factor = jnp.minimum(1.0, limit / jnp.sqrt(total + 1e-06))
    own_rows = first_ref.shape[1]
    mine = factor * full[:, pl.ds(pl.multiple_of(member * own_rows, own_rows), own_rows), :]
    new_first_ref[...] = 0.5 * first_ref[...] + 0.5 * mine
    new_second_ref[...] = 0.9 * second_ref[...] + 0.1 * mine * mine
    for dc, dx, k, columns, low in pieces:
        for dr in range(2):
            mom = core_moms[dx, k, dr] if dc else moms[dx, k, dr]
            row = ((chip ^ k) * 2 + (core ^ dc ^ dr)) * own_rows
            rows = pl.ds(pl.multiple_of(row, own_rows), own_rows)
            grad = factor * full[:, rows, columns]
            first = 0.5 * mom[0].astype(F32) + 0.5 * grad
            second = 0.9 * mom[1].astype(F32) + 0.1 * grad * grad
            stepped[:, rows, columns] = first / (jnp.sqrt(second) + 1e-08)
    basis = basis_ref[...]
    high = basis.astype(BF)
    rest = (basis - high.astype(F32)).astype(BF)
    for i in range(upd_ref.shape[0]):
        step = stepped[i].astype(BF)
        upd_ref[i] = dot(high, step) + dot(rest, step)


def local(sizes, tokens, cotangent, w_gate, w_up, w_down, basis, first_moment, second_moment):
    groups, members = sizes
    chips = members // 2
    toks, width = tokens.shape
    depth, hidden_size = w_gate.shape
    rank = basis.shape[1]
    unit, half = hidden_size // 4, rank // 2
    own_rows = first_moment.shape[1]
    limit = math.sqrt(first_moment.shape[0] * rank * hidden_size)

    def by_member(value, bits):
        return lax.ppermute(value, "member", [(i, i ^ bits) for i in range(members)])

    def by_group(value, bits):
        return lax.ppermute(value, "group", [(i, i ^ bits) for i in range(groups)])

    def by_chip(value, bits):
        pairs = []
        for g in range(groups):
            for i in range(members):
                j = i ^ bits ^ ((g // 2) % 2)
                pairs.append((g * members + i, g * members + j))
        return lax.ppermute(value, ("group", "member"), pairs)

    side, high, chip, core, member = places()

    def cut(value, column, size):
        return lax.dynamic_slice_in_dim(value, column, size, axis=value.ndim - 1)

    low_basis = basis.astype(BF)

    def block_a(which):
        return jnp.concatenate(
            [cut(w_down, (2 * side + which) * unit, unit), cut(low_basis, which * half, half)],
            axis=1,
        )

    def block_b(which):
        column = (2 * side + which) * unit
        return jnp.concatenate([cut(w_gate, column, unit), cut(w_up, column, unit)], axis=1)

    def spread(block):
        sent = block(core ^ high)
        near = {}
        for k in range(1, chips):
            bit = k & -k
            near[k] = by_chip(sent, 2 * k) if k == bit else by_member(near[k ^ bit], 2 * bit)
        far = {k: by_group(near[k], 2) for k in near}
        out = [block(core), by_member(block(1 - core), 1)]
        for k in range(1, chips):
            out += [near[k], far[k]]
        return out

    cot_x = by_group(cotangent, 1)
    blocks_a = spread(block_a)
    tok_x = by_group(tokens, 1)
    blocks_b = spread(block_b)
    cot_c, tok_c = by_member(cotangent, 1), by_member(tokens, 1)
    cot_xc, tok_xc = by_member(cot_x, 1), by_member(tok_x, 1)
    token_blocks = (tokens, tok_c, tok_x, tok_xc)
    cot_blocks = (cotangent, cot_c, cot_x, cot_xc)

    moments = jnp.stack([first_moment, second_moment]).astype(BF)
    mom_mine = cut(moments, (2 * side + core) * unit, unit)
    mom_core = by_member(cut(moments, (2 * side + 1 - core) * unit, unit), 1)
    mom_chip = jnp.stack([mom_mine, mom_core])
    mom_half = jnp.stack([mom_chip] + [by_member(mom_chip, 2 * k) for k in range(1, chips)])
    moms = jnp.stack([mom_half, by_group(mom_half, 1)])
    core_moms = by_member(moms, 1)

    four = 4 * toks
    dhid, proj = call(
        functools.partial(first_kernel, members),
        [((four, unit), F32), ((four, 2 * half), BF)],
        [pltpu.VMEM((width, unit + half), BF)],
        2 * four * width * (2 * half + unit),
        *token_blocks,
        *cot_blocks,
        *blocks_a,
    )
    proj_core = by_member(proj, 1)
    height = rank // chips
    piece = (3, height, unit)
    dgu, *lows = call(
        functools.partial(second_kernel, members),
        [((four, 2 * unit), BF)] + [(piece, BF if k else F32) for k in range(chips)],
        [pltpu.VMEM((3, rank, unit), F32), pltpu.VMEM((width, 2 * unit), BF)],
        2 * four * (width * 2 * unit + 3 * rank * unit),
        *token_blocks,
        *blocks_b,
        dhid,
        proj,
        proj_core,
    )
    share = lows[0]
    for k in range(1, chips):
        share = share + by_member(lows[k], 2 * k).astype(F32)
    bit = 2
    while bit < groups:
        sent = share.astype(BF)
        share = sent.astype(F32) + by_group(sent, bit).astype(F32)
        bit *= 2
    share = share.astype(BF)

    keep_0, keep_1, send_0, send_1 = call(
        functools.partial(grad_kernel, members),
        [((toks, width), F32)] * 2 + [((toks, width), BF)] * 2,
        [pltpu.VMEM((width, 2 * unit), BF)],
        2 * four * width * 2 * unit,
        dgu,
        *blocks_b,
    )
    near_part = keep_1 + by_member(send_1, 1).astype(F32)
    mine_part = keep_0 + by_member(send_0, 1).astype(F32)
    input_grad = (mine_part + by_group(near_part.astype(BF), 1).astype(F32)).astype(BF)

    low_mine = jnp.stack([share] + [by_member(share, 2 * k) for k in range(1, chips)])
    low_side = by_group(low_mine, 1)
    low_core = by_member(jnp.stack([low_mine, low_side]), 1)
    new_first, new_second, updates = call(
        functools.partial(last_kernel, chips, limit),
        [(first_moment.shape, F32), (second_moment.shape, F32), ((3, depth, hidden_size), F32)],
        [pltpu.VMEM((3, rank, hidden_size), F32)] * 2,
        4 * 3 * depth * rank * hidden_size,
        low_mine,
        low_side,
        low_core,
        moms,
        core_moms,
        basis,
        first_moment,
        second_moment,
    )
    return (input_grad, new_first, new_second, updates)


def solution(mesh):
    sizes = (mesh.shape["group"], mesh.shape["member"])
    tokens = P(("group", "member"), None)
    rows = P("member", None)
    low = P(None, "member", None)
    return jax.shard_map(
        functools.partial(local, sizes),
        mesh=mesh,
        in_specs=(tokens, tokens, rows, rows, rows, rows, low, low),
        out_specs=(tokens, low, low, low),
        check_vma=False,
    )
```

```python
import functools
import math

import jax
import jax.numpy as jnp
from jax import lax
from jax.experimental import pallas as pl
from jax.experimental.pallas import tpu as pltpu
from jax.sharding import PartitionSpec as P

BF = jnp.bfloat16
F32 = jnp.float32
ROWS = (((0,), (0,)), ((), ()))
COLS = (((1,), (1,)), ((), ()))


def dot(left, right, dims=(((1,), (0,)), ((), ()))):
    return lax.dot_general(left, right, dims, preferred_element_type=F32)


def call(body, outs, scratch, flops, *operands, space=pltpu.VMEM, mib=40):
    moved = sum(o.size * o.dtype.itemsize for o in operands)
    moved += sum(math.prod(s) * jnp.dtype(d).itemsize for s, d in outs)
    return pl.pallas_call(
        body,
        out_shape=[jax.ShapeDtypeStruct(s, d) for s, d in outs],
        in_specs=[pl.BlockSpec(memory_space=space)] * len(operands),
        out_specs=[pl.BlockSpec(memory_space=pltpu.VMEM)] * len(outs),
        scratch_shapes=scratch,
        compiler_params=pltpu.CompilerParams(vmem_limit_bytes=mib * 1024 * 1024),
        cost_estimate=pl.CostEstimate(
            flops=flops, bytes_accessed=moved, transcendentals=0
        ),
    )(*operands)


def places():
    group, member = lax.axis_index("group"), lax.axis_index("member")
    return group % 2, (group // 2) % 2, member // 2, member % 2, member


def sources(count):
    _, high, _, _, member = places()
    order = [member, member ^ 1]
    for k in range(1, count // 2):
        near = member ^ (2 * k) ^ high
        order += [near, near ^ 1]
    return order


def pack_kernel(parts, *refs):
    down_hbm, gate_hbm, up_hbm, basis_hbm, *moment_hbms, tok_hbm, cot_hbm = refs[:8]
    own_ref, sent_ref, core_ref, mom_ref, both_ref = refs[8:13]
    basis_ref, first_ref, second_ref, sems = refs[13:]
    toks = tok_hbm.shape[0]
    side, high, _, core, _ = places()
    depth, hidden = gate_hbm.shape
    unit, half = hidden // 4, basis_ref.shape[1] // 2
    own_rows = first_ref.shape[1]
    copies = []

    def start(source, target):
        copy = pltpu.make_async_copy(source, target, sems.at[len(copies)])
        copy.start()
        copies.append(copy)

    start(basis_hbm, basis_ref)
    start(moment_hbms[0], first_ref)
    start(moment_hbms[1], second_ref)
    targets = ((core ^ high, sent_ref), (core, own_ref), (1 - core, core_ref.at[:depth]))
    for which, ref in targets:
        column = pl.ds(pl.multiple_of((2 * side + which) * unit, unit), unit)
        for i, source in enumerate((down_hbm, gate_hbm, up_hbm)):
            lane = half + i * unit
            start(source.at[:, column], ref.at[:, lane : lane + unit])
    start(tok_hbm, both_ref.at[:toks])
    start(cot_hbm, both_ref.at[toks:])
    for copy in copies[:3]:
        copy.wait()
    for which, ref in targets:
        ranks = pl.ds(pl.multiple_of(which * half, half), half)
        ref[:, :half] = basis_ref[:, ranks].astype(BF)
    for which, ref in ((core, mom_ref), (1 - core, core_ref.at[depth:])):
        column = pl.ds(pl.multiple_of((2 * side + which) * unit, unit), unit)
        for f, source in enumerate((first_ref, second_ref)):
            rows = slice(f * own_rows, (f + 1) * own_rows)
            for i in range(parts):
                ref[rows, i * unit : (i + 1) * unit] = source[i, :, column].astype(BF)
    for copy in copies[3:]:
        copy.wait()


def joined(refs, rows):
    return jnp.concatenate([ref[rows, :] for ref in refs], axis=0)


def place_blocks(members, layout, refs, depth, full):
    for src, (which, row) in zip(sources(members), layout):
        at = pl.ds(pl.multiple_of(src * depth, depth), depth)
        full[at, :] = refs[which][row : row + depth, :]


def first_kernel(members, layout, depth, half, *refs):
    boths, blocks = refs[:4], refs[4:-4]
    toks = boths[0].shape[0] // 2
    proj_ref, dgu_ref, hidden_ref, full = refs[-4:]
    unit = hidden_ref.shape[1]
    place_blocks(members, layout, blocks, depth, full)
    tok, cot = joined(boths, slice(0, toks)), joined(boths, slice(toks, 2 * toks))
    from_cot = dot(cot, full[:, : half + unit])
    dhid = from_cot[:, half:]
    proj_ref[:, half:] = from_cot[:, :half].astype(BF)
    total = dot(tok, full[:, half + unit :])
    gate, up = total[:, :unit], total[:, unit:]
    sig = 1.0 / (1.0 + jnp.exp(-gate))
    silu = gate * sig
    hidden_ref[...] = (silu * up).astype(BF)
    dgu_ref[:, :unit] = (dhid * up * sig * (1.0 + gate * (1.0 - sig))).astype(BF)
    dgu_ref[:, unit:] = (dhid * silu).astype(BF)
    proj_ref[:, :half] = dot(tok, full[:, :half]).astype(BF)


def second_kernel(mine_ref, other_ref, dgu_ref, hidden_ref, *refs):
    *low_refs, low = refs
    unit = hidden_ref.shape[1]
    half = mine_ref.shape[1] // 2
    _, _, chip, core, _ = places()
    toks = mine_ref.shape[0] // 4
    dgu, hidden = dgu_ref[...], hidden_ref[...]
    other = jnp.concatenate(
        [other_ref[i * toks : (i + 1) * toks, :] for i in (1, 0, 3, 2)], axis=0
    )
    for away, proj in enumerate((mine_ref[...], other)):
        rows = pl.ds(away * half, half)
        tok_low = dot(proj[:, :half], dgu, ROWS)
        low[0, rows, :] = tok_low[:, :unit]
        low[1, rows, :] = tok_low[:, unit:]
        low[2, rows, :] = dot(proj[:, half:], hidden, ROWS)
    height = low_refs[0].shape[1]
    for k, ref in enumerate(low_refs):
        row = (chip ^ k) * height
        row = (row // half ^ core) * half + row % half
        rows = pl.ds(pl.multiple_of(row, height), height)
        for i in range(ref.shape[0]):
            ref[i] = low[i, rows, :].astype(ref.dtype)


def grad_kernel(dgu_ref, full_ref, keep_0, keep_1, send_0, send_1):
    toks = keep_0.shape[0]
    width = dgu_ref.shape[1]
    for i, ref in enumerate((keep_0, send_0, keep_1, send_1)):
        part = dot(dgu_ref[i * toks : (i + 1) * toks, :], full_ref[:, -width:], COLS)
        ref[...] = part.astype(ref.dtype)


def mirrored(value, size):
    out = 0
    while size > 1:
        out, value, size = out * 2 + value % 2, value // 2, size // 2
    return out


def last_kernel(chips, limit, *refs):
    lows, core_low, moms, core_moms = refs[:2], refs[2], refs[3:5], refs[5]
    basis_ref, first_ref, second_ref, new_first_ref, new_second_ref, upd_ref = refs[6:12]
    full, stepped = refs[12:]
    side, _, chip, core, member = places()
    height, unit = lows[0].shape[2:]
    squares = None
    for dc in range(2):
        for dx in range(2):
            column = ((side ^ dx) * 2 + (core ^ dc)) * unit
            columns = pl.ds(pl.multiple_of(column, unit), unit)
            for k in range(chips):
                low = (core_low[dx, k] if dc else lows[dx][k]).astype(F32)
                square = jnp.sum(low * low, axis=(0, 1), keepdims=True)
                squares = square if squares is None else squares + square
                rows = pl.ds(pl.multiple_of((chip ^ k) * height, height), height)
                full[:, rows, columns] = low
    total = jnp.sum(squares, axis=2, keepdims=True)
    factor = jnp.minimum(1.0, limit / jnp.sqrt(total + 1e-06))
    own_rows = first_ref.shape[1]
    mine = factor * full[:, pl.ds(pl.multiple_of(member * own_rows, own_rows), own_rows), :]
    new_first_ref[...] = 0.5 * first_ref[...] + 0.5 * mine
    new_second_ref[...] = 0.9 * second_ref[...] + 0.1 * mine * mine
    parts = first_ref.shape[0]
    for dc in range(2):
        for dx in range(2):
            column = ((side ^ dx) * 2 + (core ^ dc)) * unit
            columns = pl.ds(pl.multiple_of(column, unit), unit)
            for n, dr in ((n, dr) for n in range(chips) for dr in range(2)):
                row = ((chip ^ mirrored(n, chips)) * 2 + (core ^ dc ^ dr)) * own_rows
                rows = pl.ds(pl.multiple_of(row, own_rows), own_rows)
                for i in range(parts):
                    mom = []
                    for f in range(2):
                        where = pl.ds(f * own_rows, own_rows)
                        lanes = slice(i * unit, (i + 1) * unit)
                        ref = core_moms.at[dx] if dc else moms[dx]
                        mom.append(ref[n, dr, where, lanes].astype(F32))
                    grad = factor[0] * full[i, rows, columns]
                    first = 0.5 * mom[0] + 0.5 * grad
                    second = 0.9 * mom[1] + 0.1 * grad * grad
                    stepped[i, rows, columns] = first / (jnp.sqrt(second) + 1e-08)
    basis = basis_ref[...]
    high = basis.astype(BF)
    rest = (basis - high.astype(F32)).astype(BF)
    for i in range(upd_ref.shape[0]):
        step = stepped[i].astype(BF)
        upd_ref[i] = dot(high, step) + dot(rest, step)


def local(sizes, tokens, cotangent, w_gate, w_up, w_down, basis, first_moment, second_moment):
    groups, members = sizes
    chips = members // 2
    toks, width = tokens.shape
    depth, hidden_size = w_gate.shape
    rank = basis.shape[1]
    unit, half = hidden_size // 4, rank // 2
    own_rows = first_moment.shape[1]
    limit = math.sqrt(first_moment.shape[0] * rank * hidden_size)

    def by_member(value, bits):
        return lax.ppermute(value, "member", [(i, i ^ bits) for i in range(members)])

    def by_group(value, bits):
        return lax.ppermute(value, "group", [(i, i ^ bits) for i in range(groups)])

    def by_chip(value, bits):
        pairs = []
        for g in range(groups):
            for i in range(members):
                j = i ^ bits ^ ((g // 2) % 2)
                pairs.append((g * members + i, g * members + j))
        return lax.ppermute(value, ("group", "member"), pairs)

    parts = first_moment.shape[0]
    block = half + 3 * unit
    own, sent, to_core, mom_mine, both = call(
        functools.partial(pack_kernel, parts),
        [((depth, block), BF)] * 2
        + [((depth + 2 * own_rows, block), BF), ((2 * own_rows, parts * unit), BF), ((2 * toks, width), BF)],
        [
            pltpu.VMEM(basis.shape, F32),
            pltpu.VMEM(first_moment.shape, F32),
            pltpu.VMEM(second_moment.shape, F32),
            pltpu.SemaphoreType.DMA((14,)),
        ],
        0,
        w_down,
        w_gate,
        w_up,
        basis,
        first_moment,
        second_moment,
        tokens,
        cotangent,
        space=pltpu.HBM,
        mib=60,
    )
    direct = [k for k in range(1, chips) if k & (k - 1) == 0]
    passed = [k for k in range(1, chips) if k & (k - 1)]
    ordered = lax.optimization_barrier

    both_x = by_group(both, 1)
    near = {k: by_chip(sent, 2 * k) for k in reversed(direct)}
    from_core = by_member(to_core, 1)
    near, from_core, both = ordered((near, from_core, both))

    far = [by_group(jnp.concatenate([near[k] for k in direct]), 2)]
    for k in passed:
        near[k] = by_member(near[k & (k - 1)], 2 * (k & -k))
    moms = jnp.stack([mom_mine, from_core[depth:, : parts * unit]])[None]
    for bit in reversed(direct[1:]):
        moms = jnp.concatenate([moms, by_member(moms, 2 * bit)])
    both_x, both, far, near, moms = ordered((both_x, both, far, near, moms))

    far.append(by_group(jnp.concatenate([near[k] for k in passed]), 2))
    both_c = by_member(both, 1)
    both_xc = by_member(both_x, 1)
    moms = jnp.concatenate([moms, by_member(moms, 2)])
    far, both_c, both_xc, moms = ordered((far, both_c, both_xc, moms))

    layout = [(0, 0), (1, 0)]
    for k in range(1, chips):
        i = 0 if k in direct else 1
        layout += [(1 + k, 0), (1 + chips + i, (direct, passed)[i].index(k) * depth)]
    four = 4 * toks
    proj, dgu, hidden, full = call(
        functools.partial(first_kernel, members, tuple(layout), depth, half),
        [
            ((four, 2 * half), BF),
            ((four, 2 * unit), BF),
            ((four, unit), BF),
            ((width, block), BF),
        ],
        [],
        2 * four * width * (2 * half + 3 * unit),
        *(both, both_c, both_x, both_xc),
        *(own, from_core, *(near[k] for k in range(1, chips)), *far),
    )
    proj_core = by_member(proj, 1)
    moms_x = by_group(moms, 1)
    keep_0, keep_1, send_0, send_1 = call(
        grad_kernel,
        [((toks, width), F32)] * 2 + [((toks, width), BF)] * 2,
        [],
        2 * four * width * 2 * unit,
        dgu,
        full,
    )
    proj_core, send_1 = ordered((proj_core, send_1))
    near_part = by_member(send_1, 1)
    height = rank // chips
    piece = (parts, height, unit)
    lows = call(
        second_kernel,
        [(piece, BF if k else F32) for k in range(chips)],
        [pltpu.VMEM((parts, rank, unit), F32)],
        2 * four * 3 * rank * unit,
        proj,
        proj_core,
        dgu,
        hidden,
    )
    near_part = (keep_1 + near_part.astype(F32)).astype(BF)
    lows, near_part = ordered((lows, near_part))
    arrived = [by_member(lows[k], 2 * k) for k in range(1, chips)]
    arrived, moms_x = ordered((arrived, moms_x))
    core_moms = by_member(jnp.stack([moms, moms_x]), 1)
    grad_side = by_group(near_part, 1)
    share = lows[0]
    for low in arrived:
        share = share + low.astype(F32)
    bit = 2
    while bit < groups:
        sent = share.astype(BF)
        came = by_group(sent, bit)
        share = sent.astype(F32) + came.astype(F32)
        bit *= 2
    share = share.astype(BF)

    low_mine = [share] + [by_member(share, 2 * k) for k in range(1, chips)]
    low_mine, grad_side = ordered((low_mine, grad_side))
    low_mine = jnp.stack(low_mine)
    low_side = by_group(low_mine, 1)
    mine_part = keep_0 + by_member(send_0, 1).astype(F32)
    input_grad = (mine_part + grad_side.astype(F32)).astype(BF)
    low_core = by_member(jnp.stack([low_mine, low_side]), 1)
    new_first, new_second, updates = call(
        functools.partial(last_kernel, chips, limit),
        [(first_moment.shape, F32), (second_moment.shape, F32), ((3, depth, hidden_size), F32)],
        [pltpu.VMEM((3, rank, hidden_size), F32)] * 2,
        4 * 3 * depth * rank * hidden_size,
        low_mine,
        low_side,
        low_core,
        moms,
        moms_x,
        core_moms,
        basis,
        first_moment,
        second_moment,
    )
    return (input_grad, new_first, new_second, updates)


def solution(mesh):
    sizes = (mesh.shape["group"], mesh.shape["member"])
    tokens = P(("group", "member"), None)
    rows = P("member", None)
    low = P(None, "member", None)
    return jax.shard_map(
        functools.partial(local, sizes),
        mesh=mesh,
        in_specs=(tokens, tokens, rows, rows, rows, rows, low, low),
        out_specs=(tokens, low, low, low),
        check_vma=False,
    )
```

```python
import functools
import math

import jax
import jax.numpy as jnp
from jax import lax
from jax.experimental import pallas as pl
from jax.experimental.pallas import tpu as pltpu
from jax.sharding import PartitionSpec as P

BF = jnp.bfloat16
F32 = jnp.float32
ROWS = (((0,), (0,)), ((), ()))
COLS = (((1,), (1,)), ((), ()))


def dot(left, right, dims=(((1,), (0,)), ((), ()))):
    return lax.dot_general(left, right, dims, preferred_element_type=F32)


def call(body, outs, scratch, flops, *operands, pinned=False, mib=40):
    if pinned:
        operands = [pltpu.with_memory_space_constraint(o, pltpu.HBM) for o in operands]
    moved = sum(o.size * o.dtype.itemsize for o in operands)
    moved += sum(math.prod(s) * jnp.dtype(d).itemsize for s, d in outs)
    return pl.pallas_call(
        body,
        out_shape=[(pltpu.VMEM if pinned else jax.ShapeDtypeStruct)(s, d) for s, d in outs],
        in_specs=[pl.BlockSpec(memory_space=pltpu.HBM if pinned else pltpu.VMEM)] * len(operands),
        out_specs=[pl.BlockSpec(memory_space=pltpu.VMEM)] * len(outs),
        scratch_shapes=scratch,
        compiler_params=pltpu.CompilerParams(vmem_limit_bytes=mib * 1024 * 1024),
        cost_estimate=pl.CostEstimate(
            flops=flops, bytes_accessed=moved, transcendentals=0
        ),
    )(*operands)


def places():
    group, member = lax.axis_index("group"), lax.axis_index("member")
    return group % 2, (group // 2) % 2, member // 2, member % 2, member


def sources(count):
    _, high, _, _, member = places()
    order = [member, member ^ 1]
    for k in range(1, count // 2):
        near = member ^ (2 * k) ^ high
        order += [near, near ^ 1]
    return order


def pack_kernel(parts, *refs):
    down_hbm, gate_hbm, up_hbm, basis_hbm, *moment_hbms, tok_hbm, cot_hbm = refs[:8]
    own_ref, sent_ref, core_ref, mom_ref, both_ref = refs[8:13]
    basis_ref, first_ref, second_ref, sems = refs[13:]
    toks = tok_hbm.shape[0]
    side, high, _, core, _ = places()
    depth, hidden = gate_hbm.shape
    unit, half = hidden // 4, basis_ref.shape[1] // 2
    own_rows = first_ref.shape[1]
    copies = []

    def start(source, target):
        copy = pltpu.make_async_copy(source, target, sems.at[len(copies)])
        copy.start()
        copies.append(copy)

    start(basis_hbm, basis_ref)
    start(moment_hbms[0], first_ref)
    start(moment_hbms[1], second_ref)
    targets = ((core ^ high, sent_ref), (core, own_ref), (1 - core, core_ref.at[:depth]))
    for which, ref in targets:
        column = pl.ds(pl.multiple_of((2 * side + which) * unit, unit), unit)
        for i, source in enumerate((down_hbm, gate_hbm, up_hbm)):
            lane = half + i * unit
            start(source.at[:, column], ref.at[:, lane : lane + unit])
    start(tok_hbm, both_ref.at[:toks])
    start(cot_hbm, both_ref.at[toks:])
    for copy in copies[:3]:
        copy.wait()
    for which, ref in targets:
        ranks = pl.ds(pl.multiple_of(which * half, half), half)
        ref[:, :half] = basis_ref[:, ranks].astype(BF)
    for which, ref in ((core, mom_ref), (1 - core, core_ref.at[depth:])):
        column = pl.ds(pl.multiple_of((2 * side + which) * unit, unit), unit)
        for f, source in enumerate((first_ref, second_ref)):
            rows = slice(f * own_rows, (f + 1) * own_rows)
            for i in range(parts):
                ref[rows, i * unit : (i + 1) * unit] = source[i, :, column].astype(BF)
    for copy in copies[3:]:
        copy.wait()


def joined(refs, rows):
    return jnp.concatenate([ref[rows, :] for ref in refs], axis=0)


def place_blocks(members, layout, refs, depth, full):
    for src, (which, row) in zip(sources(members), layout):
        at = pl.ds(pl.multiple_of(src * depth, depth), depth)
        full[at, :] = refs[which][row : row + depth, :]


def first_kernel(members, layout, depth, half, *refs):
    boths, blocks = refs[:4], refs[4:-4]
    toks = boths[0].shape[0] // 2
    proj_ref, dgu_ref, hidden_ref, full = refs[-4:]
    unit = hidden_ref.shape[1]
    place_blocks(members, layout, blocks, depth, full)
    tok, cot = joined(boths, slice(0, toks)), joined(boths, slice(toks, 2 * toks))
    from_cot = dot(cot, full[:, : half + unit])
    dhid = from_cot[:, half:]
    proj_ref[:, half:] = from_cot[:, :half].astype(BF)
    total = dot(tok, full[:, half + unit :])
    gate, up = total[:, :unit], total[:, unit:]
    sig = 1.0 / (1.0 + jnp.exp(-gate))
    silu = gate * sig
    hidden_ref[...] = (silu * up).astype(BF)
    dgu_ref[:, :unit] = (dhid * up * sig * (1.0 + gate * (1.0 - sig))).astype(BF)
    dgu_ref[:, unit:] = (dhid * silu).astype(BF)
    proj_ref[:, :half] = dot(tok, full[:, :half]).astype(BF)


def second_kernel(mine_ref, other_ref, dgu_ref, hidden_ref, *refs):
    *low_refs, low = refs
    unit = hidden_ref.shape[1]
    half = mine_ref.shape[1] // 2
    _, _, chip, core, _ = places()
    toks = mine_ref.shape[0] // 4
    dgu, hidden = dgu_ref[...], hidden_ref[...]
    other = jnp.concatenate(
        [other_ref[i * toks : (i + 1) * toks, :] for i in (1, 0, 3, 2)], axis=0
    )
    for away, proj in enumerate((mine_ref[...], other)):
        rows = pl.ds(away * half, half)
        tok_low = dot(proj[:, :half], dgu, ROWS)
        low[0, rows, :] = tok_low[:, :unit]
        low[1, rows, :] = tok_low[:, unit:]
        low[2, rows, :] = dot(proj[:, half:], hidden, ROWS)
    height = low_refs[0].shape[1]
    for k, ref in enumerate(low_refs):
        row = (chip ^ k) * height
        row = (row // half ^ core) * half + row % half
        rows = pl.ds(pl.multiple_of(row, height), height)
        for i in range(ref.shape[0]):
            ref[i] = low[i, rows, :].astype(ref.dtype)


def grad_kernel(dgu_ref, full_ref, keep_0, keep_1, send_0, send_1):
    toks = keep_0.shape[0]
    width = dgu_ref.shape[1]
    for i, ref in enumerate((keep_0, send_0, keep_1, send_1)):
        part = dot(dgu_ref[i * toks : (i + 1) * toks, :], full_ref[:, -width:], COLS)
        ref[...] = part.astype(ref.dtype)


def mirrored(value, size):
    out = 0
    while size > 1:
        out, value, size = out * 2 + value % 2, value // 2, size // 2
    return out


def last_kernel(chips, limit, *refs):
    lows, core_low, moms, core_moms = refs[:2], refs[2], refs[3:5], refs[5]
    basis_ref, first_ref, second_ref, new_first_ref, new_second_ref, upd_ref = refs[6:12]
    full, stepped = refs[12:]
    side, _, chip, core, member = places()
    height, unit = lows[0].shape[2:]
    squares = None
    for dc in range(2):
        for dx in range(2):
            column = ((side ^ dx) * 2 + (core ^ dc)) * unit
            columns = pl.ds(pl.multiple_of(column, unit), unit)
            for k in range(chips):
                low = (core_low[dx, k] if dc else lows[dx][k]).astype(F32)
                square = jnp.sum(low * low, axis=(0, 1), keepdims=True)
                squares = square if squares is None else squares + square
                rows = pl.ds(pl.multiple_of((chip ^ k) * height, height), height)
                full[:, rows, columns] = low
    total = jnp.sum(squares, axis=2, keepdims=True)
    factor = jnp.minimum(1.0, limit / jnp.sqrt(total + 1e-06))
    own_rows = first_ref.shape[1]
    mine = factor * full[:, pl.ds(pl.multiple_of(member * own_rows, own_rows), own_rows), :]
    new_first_ref[...] = 0.5 * first_ref[...] + 0.5 * mine
    new_second_ref[...] = 0.9 * second_ref[...] + 0.1 * mine * mine
    parts = first_ref.shape[0]
    for dc in range(2):
        for dx in range(2):
            column = ((side ^ dx) * 2 + (core ^ dc)) * unit
            columns = pl.ds(pl.multiple_of(column, unit), unit)
            for n, dr in ((n, dr) for n in range(chips) for dr in range(2)):
                row = ((chip ^ mirrored(n, chips)) * 2 + (core ^ dc ^ dr)) * own_rows
                rows = pl.ds(pl.multiple_of(row, own_rows), own_rows)
                for i in range(parts):
                    mom = []
                    for f in range(2):
                        where = pl.ds(f * own_rows, own_rows)
                        lanes = slice(i * unit, (i + 1) * unit)
                        ref = core_moms.at[dx] if dc else moms[dx]
                        mom.append(ref[n, dr, where, lanes].astype(F32))
                    grad = factor[0] * full[i, rows, columns]
                    first = 0.5 * mom[0] + 0.5 * grad
                    second = 0.9 * mom[1] + 0.1 * grad * grad
                    stepped[i, rows, columns] = first / (jnp.sqrt(second) + 1e-08)
    basis = basis_ref[...]
    high = basis.astype(BF)
    rest = (basis - high.astype(F32)).astype(BF)
    for i in range(upd_ref.shape[0]):
        step = stepped[i].astype(BF)
        upd_ref[i] = dot(high, step) + dot(rest, step)


def local(sizes, tokens, cotangent, w_gate, w_up, w_down, basis, first_moment, second_moment):
    groups, members = sizes
    chips = members // 2
    toks, width = tokens.shape
    depth, hidden_size = w_gate.shape
    rank = basis.shape[1]
    unit, half = hidden_size // 4, rank // 2
    own_rows = first_moment.shape[1]
    limit = math.sqrt(first_moment.shape[0] * rank * hidden_size)

    def by_member(value, bits):
        return lax.ppermute(value, "member", [(i, i ^ bits) for i in range(members)])

    def by_group(value, bits):
        return lax.ppermute(value, "group", [(i, i ^ bits) for i in range(groups)])

    def by_chip(value, bits):
        pairs = []
        for g in range(groups):
            for i in range(members):
                j = i ^ bits ^ ((g // 2) % 2)
                pairs.append((g * members + i, g * members + j))
        return lax.ppermute(value, ("group", "member"), pairs)

    parts = first_moment.shape[0]
    block = half + 3 * unit
    own, sent, to_core, mom_mine, both = call(
        functools.partial(pack_kernel, parts),
        [((depth, block), BF)] * 2
        + [((depth + 2 * own_rows, block), BF), ((2 * own_rows, parts * unit), BF), ((2 * toks, width), BF)],
        [
            pltpu.VMEM(basis.shape, F32),
            pltpu.VMEM(first_moment.shape, F32),
            pltpu.VMEM(second_moment.shape, F32),
            pltpu.SemaphoreType.DMA((14,)),
        ],
        0,
        w_down,
        w_gate,
        w_up,
        basis,
        first_moment,
        second_moment,
        tokens,
        cotangent,
        pinned=True,
        mib=16,
    )
    direct = [k for k in range(1, chips) if k & (k - 1) == 0]
    passed = [k for k in range(1, chips) if k & (k - 1)]
    ordered = lax.optimization_barrier

    both_x = by_group(both, 1)
    near = {k: by_chip(sent, 2 * k) for k in reversed(direct)}
    from_core = by_member(to_core, 1)
    groups_of = [direct[:1], direct[1:], passed]

    def forward(which):
        return by_group(jnp.concatenate([near[k] for k in groups_of[which]]), 2)

    far = [forward(0), forward(1)]
    for k in passed:
        near[k] = by_member(near[k & (k - 1)], 2 * (k & -k))
    far[0], from_core = ordered((far[0], from_core))
    moms = jnp.stack([mom_mine, from_core[depth:, : parts * unit]])[None]
    for bit in reversed(direct[1:]):
        moms = jnp.concatenate([moms, by_member(moms, 2 * bit)])
    both_x, both, far, near, moms = ordered((both_x, both, far, near, moms))

    far.append(forward(2))
    both_c = by_member(both, 1)
    both_xc = by_member(both_x, 1)
    moms = jnp.concatenate([moms, by_member(moms, 2)])
    far, both_c, both_xc, moms = ordered((far, both_c, both_xc, moms))

    layout = [(0, 0), (1, 0)]
    for k in range(1, chips):
        i = [k in group for group in groups_of].index(True)
        layout += [(1 + k, 0), (1 + chips + i, groups_of[i].index(k) * depth)]
    four = 4 * toks
    proj, dgu, hidden, full = call(
        functools.partial(first_kernel, members, tuple(layout), depth, half),
        [
            ((four, 2 * half), BF),
            ((four, 2 * unit), BF),
            ((four, unit), BF),
            ((width, block), BF),
        ],
        [],
        2 * four * width * (2 * half + 3 * unit),
        *(both, both_c, both_x, both_xc),
        *(own, from_core, *(near[k] for k in range(1, chips)), *far),
    )
    proj_core = by_member(proj, 1)
    moms_x = by_group(moms, 1)
    keep_0, keep_1, send_0, send_1 = call(
        grad_kernel,
        [((toks, width), F32)] * 2 + [((toks, width), BF)] * 2,
        [],
        2 * four * width * 2 * unit,
        dgu,
        full,
    )
    proj_core, send_1 = ordered((proj_core, send_1))
    near_part = by_member(send_1, 1)
    height = rank // chips
    piece = (parts, height, unit)
    lows = call(
        second_kernel,
        [(piece, BF if k else F32) for k in range(chips)],
        [pltpu.VMEM((parts, rank, unit), F32)],
        2 * four * 3 * rank * unit,
        proj,
        proj_core,
        dgu,
        hidden,
    )
    near_part = (keep_1 + near_part.astype(F32)).astype(BF)
    lows, near_part = ordered((lows, near_part))
    arrived = [by_member(lows[k], 2 * k) for k in range(1, chips)]
    arrived, moms_x = ordered((arrived, moms_x))
    core_moms = by_member(jnp.stack([moms, moms_x]), 1)
    grad_side = by_group(near_part, 1)
    share = lows[0]
    for low in arrived:
        share = share + low.astype(F32)
    bit = 2
    while bit < groups:
        sent = share.astype(BF)
        came = by_group(sent, bit)
        share = sent.astype(F32) + came.astype(F32)
        bit *= 2
    share = share.astype(BF)

    low_mine = [share] + [by_member(share, 2 * k) for k in range(1, chips)]
    low_mine, grad_side = ordered((low_mine, grad_side))
    low_mine = jnp.stack(low_mine)
    low_side = by_group(low_mine, 1)
    mine_part = keep_0 + by_member(send_0, 1).astype(F32)
    input_grad = (mine_part + grad_side.astype(F32)).astype(BF)
    low_core = by_member(jnp.stack([low_mine, low_side]), 1)
    new_first, new_second, updates = call(
        functools.partial(last_kernel, chips, limit),
        [(first_moment.shape, F32), (second_moment.shape, F32), ((3, depth, hidden_size), F32)],
        [pltpu.VMEM((3, rank, hidden_size), F32)] * 2,
        4 * 3 * depth * rank * hidden_size,
        low_mine,
        low_side,
        low_core,
        moms,
        moms_x,
        core_moms,
        basis,
        first_moment,
        second_moment,
    )
    return (input_grad, new_first, new_second, updates)


def solution(mesh):
    sizes = (mesh.shape["group"], mesh.shape["member"])
    tokens = P(("group", "member"), None)
    rows = P("member", None)
    low = P(None, "member", None)
    return jax.shard_map(
        functools.partial(local, sizes),
        mesh=mesh,
        in_specs=(tokens, tokens, rows, rows, rows, rows, low, low),
        out_specs=(tokens, low, low, low),
        check_vma=False,
    )
```

```python
import functools
import math

import jax
import jax.numpy as jnp
from jax import lax
from jax.experimental import pallas as pl
from jax.experimental.pallas import tpu as pltpu
from jax.sharding import PartitionSpec as P

BF = jnp.bfloat16
F32 = jnp.float32
ROWS = (((0,), (0,)), ((), ()))
COLS = (((1,), (1,)), ((), ()))


def dot(left, right, dims=(((1,), (0,)), ((), ()))):
    return lax.dot_general(left, right, dims, preferred_element_type=F32)


def call(body, outs, scratch, flops, *operands, pinned=False, mib=40, results=pltpu.VMEM):
    if pinned:
        operands = [pltpu.with_memory_space_constraint(o, pltpu.HBM) for o in operands]
    moved = sum(o.size * o.dtype.itemsize for o in operands)
    moved += sum(math.prod(s) * jnp.dtype(d).itemsize for s, d in outs)
    return pl.pallas_call(
        body,
        out_shape=[(pltpu.VMEM if pinned else jax.ShapeDtypeStruct)(s, d) for s, d in outs],
        in_specs=[pl.BlockSpec(memory_space=pltpu.HBM if pinned else pltpu.VMEM)] * len(operands),
        out_specs=[pl.BlockSpec(memory_space=results)] * len(outs),
        scratch_shapes=scratch,
        compiler_params=pltpu.CompilerParams(vmem_limit_bytes=mib * 1024 * 1024),
        cost_estimate=pl.CostEstimate(
            flops=flops, bytes_accessed=moved, transcendentals=0
        ),
    )(*operands)


def places():
    group, member = lax.axis_index("group"), lax.axis_index("member")
    return group % 2, (group // 2) % 2, member // 2, member % 2, member


def sources(count):
    _, high, _, _, member = places()
    order = [member, member ^ 1]
    for k in range(1, count // 2):
        near = member ^ (2 * k) ^ high
        order += [near, near ^ 1]
    return order


def pack_kernel(parts, *refs):
    down_hbm, gate_hbm, up_hbm, basis_hbm, *moment_hbms, tok_hbm, cot_hbm = refs[:8]
    own_ref, sent_ref, core_ref, mom_ref, both_ref = refs[8:13]
    basis_ref, first_ref, second_ref, sems = refs[13:]
    toks = tok_hbm.shape[0]
    side, high, _, core, _ = places()
    depth, hidden = gate_hbm.shape
    unit, half = hidden // 4, basis_ref.shape[1] // 2
    own_rows = first_ref.shape[1]
    copies = []

    def start(source, target):
        copy = pltpu.make_async_copy(source, target, sems.at[len(copies)])
        copy.start()
        copies.append(copy)

    start(basis_hbm, basis_ref)
    start(moment_hbms[0], first_ref)
    start(moment_hbms[1], second_ref)
    targets = ((core ^ high, sent_ref), (core, own_ref), (1 - core, core_ref.at[:depth]))
    for which, ref in targets:
        column = pl.ds(pl.multiple_of((2 * side + which) * unit, unit), unit)
        for i, source in enumerate((down_hbm, gate_hbm, up_hbm)):
            lane = half + i * unit
            start(source.at[:, column], ref.at[:, lane : lane + unit])
    start(tok_hbm, both_ref.at[:toks])
    start(cot_hbm, both_ref.at[toks:])
    for copy in copies[:3]:
        copy.wait()
    for which, ref in targets:
        ranks = pl.ds(pl.multiple_of(which * half, half), half)
        ref[:, :half] = basis_ref[:, ranks].astype(BF)
    for which, ref in ((core, mom_ref), (1 - core, core_ref.at[depth:])):
        column = pl.ds(pl.multiple_of((2 * side + which) * unit, unit), unit)
        for f, source in enumerate((first_ref, second_ref)):
            rows = slice(f * own_rows, (f + 1) * own_rows)
            for i in range(parts):
                ref[rows, i * unit : (i + 1) * unit] = source[i, :, column].astype(BF)
    for copy in copies[3:]:
        copy.wait()


def joined(refs, rows):
    return jnp.concatenate([ref[rows, :] for ref in refs], axis=0)


def place_blocks(members, layout, refs, depth, full):
    for src, (which, row) in zip(sources(members), layout):
        at = pl.ds(pl.multiple_of(src * depth, depth), depth)
        full[at, :] = refs[which][row : row + depth, :]


def first_kernel(members, layout, depth, half, *refs):
    boths, blocks = refs[:4], refs[4:-4]
    toks = boths[0].shape[0] // 2
    proj_ref, dgu_ref, hidden_ref, full = refs[-4:]
    unit = hidden_ref.shape[1]
    place_blocks(members, layout, blocks, depth, full)
    tok, cot = joined(boths, slice(0, toks)), joined(boths, slice(toks, 2 * toks))
    from_cot = dot(cot, full[:, : half + unit])
    dhid = from_cot[:, half:]
    proj_ref[:, half:] = from_cot[:, :half].astype(BF)
    total = dot(tok, full[:, half + unit :])
    gate, up = total[:, :unit], total[:, unit:]
    sig = 1.0 / (1.0 + jnp.exp(-gate))
    silu = gate * sig
    hidden_ref[...] = (silu * up).astype(BF)
    dgu_ref[:, :unit] = (dhid * up * sig * (1.0 + gate * (1.0 - sig))).astype(BF)
    dgu_ref[:, unit:] = (dhid * silu).astype(BF)
    proj_ref[:, :half] = dot(tok, full[:, :half]).astype(BF)


def second_kernel(mine_ref, other_ref, dgu_ref, hidden_ref, *refs):
    *low_refs, low = refs
    unit = hidden_ref.shape[1]
    half = mine_ref.shape[1] // 2
    _, _, chip, core, _ = places()
    toks = mine_ref.shape[0] // 4
    dgu, hidden = dgu_ref[...], hidden_ref[...]
    other = jnp.concatenate(
        [other_ref[i * toks : (i + 1) * toks, :] for i in (1, 0, 3, 2)], axis=0
    )
    for away, proj in enumerate((mine_ref[...], other)):
        rows = pl.ds(away * half, half)
        tok_low = dot(proj[:, :half], dgu, ROWS)
        low[0, rows, :] = tok_low[:, :unit]
        low[1, rows, :] = tok_low[:, unit:]
        low[2, rows, :] = dot(proj[:, half:], hidden, ROWS)
    height = low_refs[0].shape[1]
    for k, ref in enumerate(low_refs):
        row = (chip ^ k) * height
        row = (row // half ^ core) * half + row % half
        rows = pl.ds(pl.multiple_of(row, height), height)
        for i in range(ref.shape[0]):
            ref[i] = low[i, rows, :].astype(ref.dtype)


def grad_kernel(dgu_ref, full_ref, keep_0, keep_1, send_0, send_1):
    toks = keep_0.shape[0]
    width = dgu_ref.shape[1]
    for i, ref in enumerate((keep_0, send_0, keep_1, send_1)):
        part = dot(dgu_ref[i * toks : (i + 1) * toks, :], full_ref[:, -width:], COLS)
        ref[...] = part.astype(ref.dtype)


def mirrored(value, size):
    out = 0
    while size > 1:
        out, value, size = out * 2 + value % 2, value // 2, size // 2
    return out


def last_kernel(chips, limit, *refs):
    lows, core_low, moms, core_moms = refs[:2], refs[2], refs[3:5], refs[5]
    basis_ref, first_ref, second_ref, *out_hbms = refs[6:12]
    full, stepped, new_first_ref, new_second_ref, products, sems = refs[12:]
    side, _, chip, core, member = places()
    height, unit = lows[0].shape[2:]
    squares = None
    for dc in range(2):
        for dx in range(2):
            column = ((side ^ dx) * 2 + (core ^ dc)) * unit
            columns = pl.ds(pl.multiple_of(column, unit), unit)
            for k in range(chips):
                low = (core_low[dx, k] if dc else lows[dx][k]).astype(F32)
                square = jnp.sum((low * low).reshape(-1, 8, unit), axis=0)
                squares = square if squares is None else squares + square
                rows = pl.ds(pl.multiple_of((chip ^ k) * height, height), height)
                full[:, rows, columns] = low
    total = jnp.sum(squares, axis=(0, 1), keepdims=True)
    factor = jnp.minimum(1.0, limit / jnp.sqrt(total + 1e-06))
    own_rows = first_ref.shape[1]
    parts = first_ref.shape[0]
    half, tenth = 0.5 * factor, 0.1 * factor * factor
    basis = basis_ref[...]
    high = basis.astype(BF)
    rest = (basis - high.astype(F32)).astype(BF)
    mine = pl.ds(pl.multiple_of(member * own_rows, own_rows), own_rows)
    copies = []

    def start(source, target):
        copies.append(pltpu.make_async_copy(source, target, sems.at[len(copies)]))
        copies[-1].start()

    low = full[:, mine, :]
    new_first_ref[...] = 0.5 * first_ref[...] + half * low
    new_second_ref[...] = 0.9 * second_ref[...] + tenth * low * low
    start(new_first_ref, out_hbms[0])
    start(new_second_ref, out_hbms[1])
    for i in range(parts):
        for dc in range(2):
            for dx in range(2):
                column = ((side ^ dx) * 2 + (core ^ dc)) * unit
                columns = pl.ds(pl.multiple_of(column, unit), unit)
                lanes = slice(i * unit, (i + 1) * unit)
                ref = core_moms.at[dx] if dc else moms[dx]
                for n, dr in ((n, dr) for n in range(chips) for dr in range(2)):
                    row = ((chip ^ mirrored(n, chips)) * 2 + (core ^ dc ^ dr)) * own_rows
                    rows = pl.ds(pl.multiple_of(row, own_rows), own_rows)
                    low = full[i, rows, columns]
                    first = 0.5 * ref[n, dr, :own_rows, lanes].astype(F32) + half * low
                    second = 0.9 * ref[n, dr, own_rows:, lanes].astype(F32) + tenth * low * low
                    root = second * lax.rsqrt(second) + 1e-08
                    stepped[rows, columns] = first * pl.reciprocal(root, approx=True)
        step = stepped[...].astype(BF)
        products[i] = dot(high, step) + dot(rest, step)
        start(products.at[i], out_hbms[2].at[i])
    for copy in copies:
        copy.wait()


def local(sizes, tokens, cotangent, w_gate, w_up, w_down, basis, first_moment, second_moment):
    groups, members = sizes
    chips = members // 2
    toks, width = tokens.shape
    depth, hidden_size = w_gate.shape
    rank = basis.shape[1]
    unit, half = hidden_size // 4, rank // 2
    own_rows = first_moment.shape[1]
    limit = math.sqrt(first_moment.shape[0] * rank * hidden_size)

    def by_member(value, bits):
        return lax.ppermute(value, "member", [(i, i ^ bits) for i in range(members)])

    def by_group(value, bits):
        return lax.ppermute(value, "group", [(i, i ^ bits) for i in range(groups)])

    def by_chip(value, bits):
        pairs = []
        for g in range(groups):
            for i in range(members):
                j = i ^ bits ^ ((g // 2) % 2)
                pairs.append((g * members + i, g * members + j))
        return lax.ppermute(value, ("group", "member"), pairs)

    parts = first_moment.shape[0]
    block = half + 3 * unit
    own, sent, to_core, mom_mine, both = call(
        functools.partial(pack_kernel, parts),
        [((depth, block), BF)] * 2
        + [((depth + 2 * own_rows, block), BF), ((2 * own_rows, parts * unit), BF), ((2 * toks, width), BF)],
        [
            pltpu.VMEM(basis.shape, F32),
            pltpu.VMEM(first_moment.shape, F32),
            pltpu.VMEM(second_moment.shape, F32),
            pltpu.SemaphoreType.DMA((14,)),
        ],
        0,
        w_down,
        w_gate,
        w_up,
        basis,
        first_moment,
        second_moment,
        tokens,
        cotangent,
        pinned=True,
        mib=16,
    )
    direct = [k for k in range(1, chips) if k & (k - 1) == 0]
    passed = [k for k in range(1, chips) if k & (k - 1)]
    ordered = lax.optimization_barrier

    both_x = by_group(both, 1)
    near = {k: by_chip(sent, 2 * k) for k in reversed(direct)}
    from_core = by_member(to_core, 1)
    groups_of = [direct[:1], direct[1:], passed]

    def forward(which):
        return by_group(jnp.concatenate([near[k] for k in groups_of[which]]), 2)

    far = [forward(0), forward(1)]
    for k in passed:
        near[k] = by_member(near[k & (k - 1)], 2 * (k & -k))
    far[0], from_core = ordered((far[0], from_core))
    moms = jnp.stack([mom_mine, from_core[depth:, : parts * unit]])[None]
    for bit in reversed(direct[1:]):
        moms = jnp.concatenate([moms, by_member(moms, 2 * bit)])
    both_x, both, far, near, moms = ordered((both_x, both, far, near, moms))

    far.append(forward(2))
    both_c = by_member(both, 1)
    both_xc = by_member(both_x, 1)
    moms = jnp.concatenate([moms, by_member(moms, 2)])
    far, both_c, both_xc, moms = ordered((far, both_c, both_xc, moms))

    layout = [(0, 0), (1, 0)]
    for k in range(1, chips):
        i = [k in group for group in groups_of].index(True)
        layout += [(1 + k, 0), (1 + chips + i, groups_of[i].index(k) * depth)]
    four = 4 * toks
    proj, dgu, hidden, full = call(
        functools.partial(first_kernel, members, tuple(layout), depth, half),
        [
            ((four, 2 * half), BF),
            ((four, 2 * unit), BF),
            ((four, unit), BF),
            ((width, block), BF),
        ],
        [],
        2 * four * width * (2 * half + 3 * unit),
        *(both, both_c, both_x, both_xc),
        *(own, from_core, *(near[k] for k in range(1, chips)), *far),
    )
    proj_core = by_member(proj, 1)
    moms_x = by_group(moms, 1)
    keep_0, keep_1, send_0, send_1 = call(
        grad_kernel,
        [((toks, width), F32)] * 2 + [((toks, width), BF)] * 2,
        [],
        2 * four * width * 2 * unit,
        dgu,
        full,
    )
    proj_core, send_1 = ordered((proj_core, send_1))
    near_part = by_member(send_1, 1)
    height = rank // chips
    piece = (parts, height, unit)
    lows = call(
        second_kernel,
        [(piece, BF if k else F32) for k in range(chips)],
        [pltpu.VMEM((parts, rank, unit), F32)],
        2 * four * 3 * rank * unit,
        proj,
        proj_core,
        dgu,
        hidden,
    )
    near_part = (keep_1 + near_part.astype(F32)).astype(BF)
    lows, near_part = ordered((lows, near_part))
    arrived = [by_member(lows[k], 2 * k) for k in range(1, chips)]
    arrived, moms_x = ordered((arrived, moms_x))
    core_moms = by_member(jnp.stack([moms, moms_x]), 1)
    grad_side = by_group(near_part, 1)
    share = lows[0]
    for low in arrived:
        share = share + low.astype(F32)
    bit = 2
    while bit < groups:
        sent = share.astype(BF)
        came = by_group(sent, bit)
        share = sent.astype(F32) + came.astype(F32)
        bit *= 2
    share = share.astype(BF)

    low_mine = [share] + [by_member(share, 2 * k) for k in range(1, chips)]
    low_mine, grad_side = ordered((low_mine, grad_side))
    low_mine = jnp.stack(low_mine)
    low_side = by_group(low_mine, 1)
    mine_part = keep_0 + by_member(send_0, 1).astype(F32)
    input_grad = (mine_part + grad_side.astype(F32)).astype(BF)
    low_core = by_member(jnp.stack([low_mine, low_side]), 1)
    new_first, new_second, updates = call(
        functools.partial(last_kernel, chips, limit),
        [(first_moment.shape, F32), (second_moment.shape, F32), ((parts, depth, hidden_size), F32)],
        [
            pltpu.VMEM((parts, rank, hidden_size), F32),
            pltpu.VMEM((rank, hidden_size), F32),
            pltpu.VMEM(first_moment.shape, F32),
            pltpu.VMEM(second_moment.shape, F32),
            pltpu.VMEM((parts, depth, hidden_size), F32),
            pltpu.SemaphoreType.DMA((parts + 2,)),
        ],
        4 * 3 * depth * rank * hidden_size,
        low_mine,
        low_side,
        low_core,
        moms,
        moms_x,
        core_moms,
        basis,
        first_moment,
        second_moment,
        results=pltpu.HBM,
    )
    return (input_grad, new_first, new_second, updates)


def solution(mesh):
    sizes = (mesh.shape["group"], mesh.shape["member"])
    tokens = P(("group", "member"), None)
    rows = P("member", None)
    low = P(None, "member", None)
    return jax.shard_map(
        functools.partial(local, sizes),
        mesh=mesh,
        in_specs=(tokens, tokens, rows, rows, rows, rows, low, low),
        out_specs=(tokens, low, low, low),
        check_vma=False,
    )
```

```python
import functools
import math

import jax
import jax.numpy as jnp
from jax import lax
from jax.experimental import pallas as pl
from jax.experimental.pallas import tpu as pltpu
from jax.sharding import PartitionSpec as P

BF = jnp.bfloat16
F32 = jnp.float32
ROWS = (((0,), (0,)), ((), ()))
COLS = (((1,), (1,)), ((), ()))


def dot(left, right, dims=(((1,), (0,)), ((), ()))):
    return lax.dot_general(left, right, dims, preferred_element_type=F32)


def call(body, outs, scratch, flops, *operands, pinned=False, mib=40, results=pltpu.VMEM):
    if pinned:
        operands = [pltpu.with_memory_space_constraint(o, pltpu.HBM) for o in operands]
    moved = sum(o.size * o.dtype.itemsize for o in operands)
    moved += sum(math.prod(s) * jnp.dtype(d).itemsize for s, d in outs)
    return pl.pallas_call(
        body,
        out_shape=[(pltpu.VMEM if pinned else jax.ShapeDtypeStruct)(s, d) for s, d in outs],
        in_specs=[pl.BlockSpec(memory_space=pltpu.HBM if pinned else pltpu.VMEM)] * len(operands),
        out_specs=[pl.BlockSpec(memory_space=results)] * len(outs),
        scratch_shapes=scratch,
        compiler_params=pltpu.CompilerParams(vmem_limit_bytes=mib * 1024 * 1024),
        cost_estimate=pl.CostEstimate(
            flops=flops, bytes_accessed=moved, transcendentals=0
        ),
    )(*operands)


def places():
    group, member = lax.axis_index("group"), lax.axis_index("member")
    return group % 2, (group // 2) % 2, member // 2, member % 2, member


def sources(count):
    _, high, _, _, member = places()
    order = [member, member ^ 1]
    for k in range(1, count // 2):
        near = member ^ (2 * k) ^ high
        order += [near, near ^ 1]
    return order


def pack_kernel(parts, *refs):
    down_hbm, gate_hbm, up_hbm, basis_hbm, *moment_hbms, tok_hbm, cot_hbm = refs[:8]
    own_ref, sent_ref, core_ref, mom_ref, both_ref = refs[8:13]
    basis_ref, first_ref, second_ref, sems = refs[13:]
    toks = tok_hbm.shape[0]
    side, high, _, core, _ = places()
    depth, hidden = gate_hbm.shape
    unit, half = hidden // 4, basis_ref.shape[1] // 2
    own_rows = first_ref.shape[1]
    copies = []

    def start(source, target):
        copy = pltpu.make_async_copy(source, target, sems.at[len(copies)])
        copy.start()
        copies.append(copy)

    start(basis_hbm, basis_ref)
    start(moment_hbms[0], first_ref)
    start(moment_hbms[1], second_ref)
    targets = ((core ^ high, sent_ref), (core, own_ref), (1 - core, core_ref.at[:depth]))
    for which, ref in targets:
        column = pl.ds(pl.multiple_of((2 * side + which) * unit, unit), unit)
        for i, source in enumerate((down_hbm, gate_hbm, up_hbm)):
            lane = half + i * unit
            start(source.at[:, column], ref.at[:, lane : lane + unit])
    start(tok_hbm, both_ref.at[:toks])
    start(cot_hbm, both_ref.at[toks:])
    for copy in copies[:3]:
        copy.wait()
    for which, ref in targets:
        ranks = pl.ds(pl.multiple_of(which * half, half), half)
        ref[:, :half] = basis_ref[:, ranks].astype(BF)
    for which, ref in ((core, mom_ref), (1 - core, core_ref.at[depth:])):
        column = pl.ds(pl.multiple_of((2 * side + which) * unit, unit), unit)
        for f, source in enumerate((first_ref, second_ref)):
            rows = slice(f * own_rows, (f + 1) * own_rows)
            for i in range(parts):
                ref[rows, i * unit : (i + 1) * unit] = source[i, :, column].astype(BF)
    for copy in copies[3:]:
        copy.wait()


def joined(refs, rows):
    return jnp.concatenate([ref[rows, :] for ref in refs], axis=0)


def place_blocks(members, layout, refs, depth, full):
    for src, (which, row) in zip(sources(members), layout):
        at = pl.ds(pl.multiple_of(src * depth, depth), depth)
        full[at, :] = refs[which][row : row + depth, :]


def first_kernel(members, layout, depth, half, *refs):
    boths, blocks = refs[:4], refs[4:-4]
    toks = boths[0].shape[0] // 2
    proj_ref, dgu_ref, hidden_ref, full = refs[-4:]
    unit = hidden_ref.shape[1]
    place_blocks(members, layout, blocks, depth, full)
    tok, cot = joined(boths, slice(0, toks)), joined(boths, slice(toks, 2 * toks))
    from_cot = dot(cot, full[:, : half + unit])
    dhid = from_cot[:, half:]
    proj_ref[:, half:] = from_cot[:, :half].astype(BF)
    total = dot(tok, full[:, half + unit :])
    gate, up = total[:, :unit], total[:, unit:]
    sig = 1.0 / (1.0 + jnp.exp(-gate))
    silu = gate * sig
    hidden_ref[...] = (silu * up).astype(BF)
    dgu_ref[:, :unit] = (dhid * up * sig * (1.0 + gate * (1.0 - sig))).astype(BF)
    dgu_ref[:, unit:] = (dhid * silu).astype(BF)
    proj_ref[:, :half] = dot(tok, full[:, :half]).astype(BF)


def second_kernel(mine_ref, other_ref, dgu_ref, hidden_ref, *refs):
    *low_refs, low = refs
    unit = hidden_ref.shape[1]
    half = mine_ref.shape[1] // 2
    _, _, chip, core, _ = places()
    toks = mine_ref.shape[0] // 4
    dgu, hidden = dgu_ref[...], hidden_ref[...]
    other = jnp.concatenate(
        [other_ref[i * toks : (i + 1) * toks, :] for i in (1, 0, 3, 2)], axis=0
    )
    for away, proj in enumerate((mine_ref[...], other)):
        rows = pl.ds(away * half, half)
        tok_low = dot(proj[:, :half], dgu, ROWS)
        low[0, rows, :] = tok_low[:, :unit]
        low[1, rows, :] = tok_low[:, unit:]
        low[2, rows, :] = dot(proj[:, half:], hidden, ROWS)
    height = low_refs[0].shape[1]
    for k, ref in enumerate(low_refs):
        row = (chip ^ k) * height
        row = (row // half ^ core) * half + row % half
        rows = pl.ds(pl.multiple_of(row, height), height)
        for i in range(ref.shape[0]):
            ref[i] = low[i, rows, :].astype(ref.dtype)


def grad_kernel(dgu_ref, full_ref, keep_0, keep_1, send_0, send_1):
    toks = keep_0.shape[0]
    width = dgu_ref.shape[1]
    for i, ref in enumerate((keep_0, send_0, keep_1, send_1)):
        part = dot(dgu_ref[i * toks : (i + 1) * toks, :], full_ref[:, -width:], COLS)
        ref[...] = part.astype(ref.dtype)


def mirrored(value, size):
    out = 0
    while size > 1:
        out, value, size = out * 2 + value % 2, value // 2, size // 2
    return out


def last_kernel(chips, limit, *refs):
    lows, core_low, moms, core_moms = refs[:2], refs[2], refs[3:5], refs[5]
    basis_ref, first_ref, second_ref, *out_hbms = refs[6:12]
    full, stepped, new_first_ref, new_second_ref, products, sems = refs[12:]
    side, _, chip, core, member = places()
    height, unit = lows[0].shape[2:]
    squares = None
    for dc in range(2):
        for dx in range(2):
            column = ((side ^ dx) * 2 + (core ^ dc)) * unit
            columns = pl.ds(pl.multiple_of(column, unit), unit)
            for k in range(chips):
                low = (core_low[dx, k] if dc else lows[dx][k]).astype(F32)
                square = jnp.sum((low * low).reshape(-1, 8, unit), axis=0)
                squares = square if squares is None else squares + square
                rows = pl.ds(pl.multiple_of((chip ^ k) * height, height), height)
                full[:, rows, columns] = low
    total = jnp.sum(squares, axis=(0, 1), keepdims=True)
    factor = jnp.minimum(1.0, limit / jnp.sqrt(total + 1e-06))
    own_rows = first_ref.shape[1]
    parts = first_ref.shape[0]
    half, tenth = 0.5 * factor, 0.1 * factor * factor
    basis = basis_ref[...]
    high = basis.astype(BF)
    rest = (basis - high.astype(F32)).astype(BF)
    mine = pl.ds(pl.multiple_of(member * own_rows, own_rows), own_rows)
    copies = []

    def start(source, target):
        copies.append(pltpu.make_async_copy(source, target, sems.at[len(copies)]))
        copies[-1].start()

    low = full[:, mine, :]
    new_first_ref[...] = 0.5 * first_ref[...] + half * low
    new_second_ref[...] = 0.9 * second_ref[...] + tenth * low * low
    start(new_first_ref, out_hbms[0])
    start(new_second_ref, out_hbms[1])
    for i in range(parts):
        for dc in range(2):
            for dx in range(2):
                column = ((side ^ dx) * 2 + (core ^ dc)) * unit
                columns = pl.ds(pl.multiple_of(column, unit), unit)
                lanes = slice(i * unit, (i + 1) * unit)
                ref = core_moms.at[dx] if dc else moms[dx]
                for n, dr in ((n, dr) for n in range(chips) for dr in range(2)):
                    row = ((chip ^ mirrored(n, chips)) * 2 + (core ^ dc ^ dr)) * own_rows
                    rows = pl.ds(pl.multiple_of(row, own_rows), own_rows)
                    low = full[i, rows, columns]
                    first = 0.5 * ref[n, dr, :own_rows, lanes].astype(F32) + half * low
                    second = 0.9 * ref[n, dr, own_rows:, lanes].astype(F32) + tenth * low * low
                    root = second * lax.rsqrt(second) + 1e-08
                    stepped[rows, columns] = first * pl.reciprocal(root, approx=True)
        step = stepped[...].astype(BF)
        products[i] = dot(high, step) + dot(rest, step)
        start(products.at[i], out_hbms[2].at[i])
    for copy in copies:
        copy.wait()


def local(sizes, tokens, cotangent, w_gate, w_up, w_down, basis, first_moment, second_moment):
    groups, members = sizes
    chips = members // 2
    toks, width = tokens.shape
    depth, hidden_size = w_gate.shape
    rank = basis.shape[1]
    unit, half = hidden_size // 4, rank // 2
    own_rows = first_moment.shape[1]
    limit = math.sqrt(first_moment.shape[0] * rank * hidden_size)

    def by_member(value, bits):
        return lax.ppermute(value, "member", [(i, i ^ bits) for i in range(members)])

    def by_group(value, bits):
        return lax.ppermute(value, "group", [(i, i ^ bits) for i in range(groups)])

    def by_chip(value, bits):
        pairs = []
        for g in range(groups):
            for i in range(members):
                j = i ^ bits ^ ((g // 2) % 2)
                pairs.append((g * members + i, g * members + j))
        return lax.ppermute(value, ("group", "member"), pairs)

    parts = first_moment.shape[0]
    block = half + 3 * unit
    own, sent, to_core, mom_mine, both = call(
        functools.partial(pack_kernel, parts),
        [((depth, block), BF)] * 2
        + [((depth + 2 * own_rows, block), BF), ((2 * own_rows, parts * unit), BF), ((2 * toks, width), BF)],
        [
            pltpu.VMEM(basis.shape, F32),
            pltpu.VMEM(first_moment.shape, F32),
            pltpu.VMEM(second_moment.shape, F32),
            pltpu.SemaphoreType.DMA((14,)),
        ],
        0,
        w_down,
        w_gate,
        w_up,
        basis,
        first_moment,
        second_moment,
        tokens,
        cotangent,
        pinned=True,
        mib=16,
    )
    direct = [k for k in range(1, chips) if k & (k - 1) == 0]
    passed = [k for k in range(1, chips) if k & (k - 1)]
    ordered = lax.optimization_barrier

    both_x = by_group(both, 1)
    near = {k: by_chip(sent, 2 * k) for k in reversed(direct)}
    from_core = by_member(to_core, 1)
    groups_of = [direct[:1], direct[1:], passed]

    def forward(which):
        return by_group(jnp.concatenate([near[k] for k in groups_of[which]]), 2)

    for k in passed:
        near[k] = by_member(near[k & (k - 1)], 2 * (k & -k))
    far = [forward(0), forward(1)]
    far[0], from_core = ordered((far[0], from_core))
    moms = jnp.stack([mom_mine, from_core[depth:, : parts * unit]])[None]
    for bit in reversed(direct[1:]):
        moms = jnp.concatenate([moms, by_member(moms, 2 * bit)])
    near, far, both_x, both, moms = ordered((near, far, both_x, both, moms))

    far.append(forward(2))
    both_c = by_member(both, 1)
    both_xc = by_member(both_x, 1)
    moms = jnp.concatenate([moms, by_member(moms, 2)])
    far, both_c, both_xc = ordered((far, both_c, both_xc))

    layout = [(0, 0), (1, 0)]
    for k in range(1, chips):
        i = [k in group for group in groups_of].index(True)
        layout += [(1 + k, 0), (1 + chips + i, groups_of[i].index(k) * depth)]
    four = 4 * toks
    proj, dgu, hidden, full = call(
        functools.partial(first_kernel, members, tuple(layout), depth, half),
        [
            ((four, 2 * half), BF),
            ((four, 2 * unit), BF),
            ((four, unit), BF),
            ((width, block), BF),
        ],
        [],
        2 * four * width * (2 * half + 3 * unit),
        *(both, both_c, both_x, both_xc),
        *(own, from_core, *(near[k] for k in range(1, chips)), *far),
    )
    dgu, moms = ordered((dgu, moms))
    proj_core = by_member(proj, 1)
    moms_x = by_group(moms, 1)
    keep_0, keep_1, send_0, send_1 = call(
        grad_kernel,
        [((toks, width), F32)] * 2 + [((toks, width), BF)] * 2,
        [],
        2 * four * width * 2 * unit,
        dgu,
        full,
    )
    proj_core, send_1 = ordered((proj_core, send_1))
    near_part = by_member(send_1, 1)
    height = rank // chips
    piece = (parts, height, unit)
    lows = call(
        second_kernel,
        [(piece, BF if k else F32) for k in range(chips)],
        [pltpu.VMEM((parts, rank, unit), F32)],
        2 * four * 3 * rank * unit,
        proj,
        proj_core,
        dgu,
        hidden,
    )
    near_part = (keep_1 + near_part.astype(F32)).astype(BF)
    lows, near_part = ordered((lows, near_part))
    arrived = [by_member(lows[k], 2 * k) for k in reversed(range(1, chips))]
    moms_x, arrived = ordered((moms_x, arrived))
    core_moms = by_member(jnp.stack([moms, moms_x]), 1)
    grad_side = by_group(near_part, 1)
    share = lows[0]
    for low in arrived:
        share = share + low.astype(F32)
    bit = 2
    while bit < groups:
        sent = share.astype(BF)
        came = by_group(sent, bit)
        share = sent.astype(F32) + came.astype(F32)
        bit *= 2
    share = share.astype(BF)

    low_mine = [by_member(share, 2 * k) for k in reversed(range(1, chips))]
    grad_side, low_mine = ordered((grad_side, low_mine))
    low_mine = jnp.stack([share] + low_mine[::-1])
    low_side = by_group(low_mine, 1)
    mine_part = keep_0 + by_member(send_0, 1).astype(F32)
    input_grad = (mine_part + grad_side.astype(F32)).astype(BF)
    low_core = by_member(jnp.stack([low_mine, low_side]), 1)
    new_first, new_second, updates = call(
        functools.partial(last_kernel, chips, limit),
        [(first_moment.shape, F32), (second_moment.shape, F32), ((parts, depth, hidden_size), F32)],
        [
            pltpu.VMEM((parts, rank, hidden_size), F32),
            pltpu.VMEM((rank, hidden_size), F32),
            pltpu.VMEM(first_moment.shape, F32),
            pltpu.VMEM(second_moment.shape, F32),
            pltpu.VMEM((parts, depth, hidden_size), F32),
            pltpu.SemaphoreType.DMA((parts + 2,)),
        ],
        4 * 3 * depth * rank * hidden_size,
        low_mine,
        low_side,
        low_core,
        moms,
        moms_x,
        core_moms,
        basis,
        first_moment,
        second_moment,
        results=pltpu.HBM,
    )
    return (input_grad, new_first, new_second, updates)


def solution(mesh):
    sizes = (mesh.shape["group"], mesh.shape["member"])
    tokens = P(("group", "member"), None)
    rows = P("member", None)
    low = P(None, "member", None)
    return jax.shard_map(
        functools.partial(local, sizes),
        mesh=mesh,
        in_specs=(tokens, tokens, rows, rows, rows, rows, low, low),
        out_specs=(tokens, low, low, low),
        check_vma=False,
    )
```

```python
import functools
import math

import jax
import jax.numpy as jnp
from jax import lax
from jax.experimental import pallas as pl
from jax.experimental.pallas import tpu as pltpu
from jax.sharding import PartitionSpec as P

BF = jnp.bfloat16
F32 = jnp.float32
ROWS = (((0,), (0,)), ((), ()))
COLS = (((1,), (1,)), ((), ()))


def dot(left, right, dims=(((1,), (0,)), ((), ()))):
    return lax.dot_general(left, right, dims, preferred_element_type=F32)


def call(body, outs, scratch, flops, *operands, pinned=False, mib=40, results=pltpu.VMEM):
    if pinned:
        operands = [pltpu.with_memory_space_constraint(o, pltpu.HBM) for o in operands]
    moved = sum(o.size * o.dtype.itemsize for o in operands)
    moved += sum(math.prod(s) * jnp.dtype(d).itemsize for s, d in outs)
    return pl.pallas_call(
        body,
        out_shape=[(pltpu.VMEM if pinned else jax.ShapeDtypeStruct)(s, d) for s, d in outs],
        in_specs=[pl.BlockSpec(memory_space=pltpu.HBM if pinned else pltpu.VMEM)] * len(operands),
        out_specs=[pl.BlockSpec(memory_space=results)] * len(outs),
        scratch_shapes=scratch,
        compiler_params=pltpu.CompilerParams(vmem_limit_bytes=mib * 1024 * 1024),
        cost_estimate=pl.CostEstimate(
            flops=flops, bytes_accessed=moved, transcendentals=0
        ),
    )(*operands)


def places():
    group, member = lax.axis_index("group"), lax.axis_index("member")
    return group % 2, (group // 2) % 2, member // 2, member % 2, member


def sources(count):
    _, high, _, _, member = places()
    order = [member, member ^ 1]
    for k in range(1, count // 2):
        near = member ^ (2 * k) ^ high
        order += [near, near ^ 1]
    return order


def pack_kernel(parts, *refs):
    down_hbm, gate_hbm, up_hbm, basis_hbm, *moment_hbms, tok_hbm, cot_hbm = refs[:8]
    own_ref, sent_ref, core_ref, mom_ref, both_ref = refs[8:13]
    basis_ref, first_ref, second_ref, sems = refs[13:]
    toks = tok_hbm.shape[0]
    side, high, _, core, _ = places()
    depth, hidden = gate_hbm.shape
    unit, half = hidden // 4, basis_ref.shape[1] // 2
    own_rows = first_ref.shape[1]
    copies = []

    def start(source, target):
        copy = pltpu.make_async_copy(source, target, sems.at[len(copies)])
        copy.start()
        copies.append(copy)

    start(basis_hbm, basis_ref)
    start(moment_hbms[0], first_ref)
    start(moment_hbms[1], second_ref)
    targets = ((core ^ high, sent_ref), (core, own_ref), (1 - core, core_ref.at[:depth]))
    for which, ref in targets:
        column = pl.ds(pl.multiple_of((2 * side + which) * unit, unit), unit)
        for i, source in enumerate((down_hbm, gate_hbm, up_hbm)):
            lane = half + i * unit
            start(source.at[:, column], ref.at[:, lane : lane + unit])
    start(tok_hbm, both_ref.at[:toks])
    start(cot_hbm, both_ref.at[toks:])
    for copy in copies[:3]:
        copy.wait()
    for which, ref in targets:
        ranks = pl.ds(pl.multiple_of(which * half, half), half)
        ref[:, :half] = basis_ref[:, ranks].astype(BF)
    for which, ref in ((core, mom_ref), (1 - core, core_ref.at[depth:])):
        column = pl.ds(pl.multiple_of((2 * side + which) * unit, unit), unit)
        for f, source in enumerate((first_ref, second_ref)):
            rows = slice(f * own_rows, (f + 1) * own_rows)
            for i in range(parts):
                ref[rows, i * unit : (i + 1) * unit] = source[i, :, column].astype(BF)
    for copy in copies[3:]:
        copy.wait()


def joined(refs, rows):
    return jnp.concatenate([ref[rows, :] for ref in refs], axis=0)


def place_blocks(members, layout, refs, depth, full):
    for src, (which, row) in zip(sources(members), layout):
        at = pl.ds(pl.multiple_of(src * depth, depth), depth)
        full[at, :] = refs[which][row : row + depth, :]


def first_kernel(members, layout, depth, half, *refs):
    boths, blocks = refs[:4], refs[4:-4]
    toks = boths[0].shape[0] // 2
    proj_ref, dgu_ref, hidden_ref, full = refs[-4:]
    unit = hidden_ref.shape[1]
    place_blocks(members, layout, blocks, depth, full)
    tok, cot = joined(boths, slice(0, toks)), joined(boths, slice(toks, 2 * toks))
    from_cot = dot(cot, full[:, : half + unit])
    dhid = from_cot[:, half:]
    proj_ref[:, half:] = from_cot[:, :half].astype(BF)
    total = dot(tok, full[:, half + unit :])
    gate, up = total[:, :unit], total[:, unit:]
    sig = 1.0 / (1.0 + jnp.exp(-gate))
    silu = gate * sig
    hidden_ref[...] = (silu * up).astype(BF)
    dgu_ref[:, :unit] = (dhid * up * sig * (1.0 + gate * (1.0 - sig))).astype(BF)
    dgu_ref[:, unit:] = (dhid * silu).astype(BF)
    proj_ref[:, :half] = dot(tok, full[:, :half]).astype(BF)


def second_kernel(mine_ref, other_ref, dgu_ref, hidden_ref, *refs):
    *low_refs, low = refs
    unit = hidden_ref.shape[1]
    half = mine_ref.shape[1] // 2
    _, _, chip, core, _ = places()
    toks = mine_ref.shape[0] // 4
    dgu, hidden = dgu_ref[...], hidden_ref[...]
    other = jnp.concatenate(
        [other_ref[i * toks : (i + 1) * toks, :] for i in (1, 0, 3, 2)], axis=0
    )
    for away, proj in enumerate((mine_ref[...], other)):
        rows = pl.ds(away * half, half)
        tok_low = dot(proj[:, :half], dgu, ROWS)
        low[0, rows, :] = tok_low[:, :unit]
        low[1, rows, :] = tok_low[:, unit:]
        low[2, rows, :] = dot(proj[:, half:], hidden, ROWS)
    height = low_refs[0].shape[1]
    for k, ref in enumerate(low_refs):
        row = (chip ^ k) * height
        row = (row // half ^ core) * half + row % half
        rows = pl.ds(pl.multiple_of(row, height), height)
        for i in range(ref.shape[0]):
            ref[i] = low[i, rows, :].astype(ref.dtype)


def grad_kernel(dgu_ref, full_ref, keep_0, keep_1, send_0, send_1):
    toks = keep_0.shape[0]
    width = dgu_ref.shape[1]
    for i, ref in enumerate((keep_0, send_0, keep_1, send_1)):
        part = dot(dgu_ref[i * toks : (i + 1) * toks, :], full_ref[:, -width:], COLS)
        ref[...] = part.astype(ref.dtype)


def mirrored(value, size):
    out = 0
    while size > 1:
        out, value, size = out * 2 + value % 2, value // 2, size // 2
    return out


def last_kernel(chips, limit, *refs):
    lows, core_lows, moms, core_moms = refs[:2], refs[2:4], refs[4:6], refs[6]
    basis_ref, first_ref, second_ref, *out_hbms = refs[7:13]
    full, stepped, new_first_ref, new_second_ref, products, sems = refs[13:]
    side, _, chip, core, member = places()
    height, unit = lows[0].shape[2:]
    squares = None
    for dc in range(2):
        for dx in range(2):
            column = ((side ^ dx) * 2 + (core ^ dc)) * unit
            columns = pl.ds(pl.multiple_of(column, unit), unit)
            for k in range(chips):
                low = (core_lows if dc else lows)[dx][k].astype(F32)
                square = jnp.sum((low * low).reshape(-1, 8, unit), axis=0)
                squares = square if squares is None else squares + square
                rows = pl.ds(pl.multiple_of((chip ^ k) * height, height), height)
                full[:, rows, columns] = low
    total = jnp.sum(squares, axis=(0, 1), keepdims=True)
    factor = jnp.minimum(1.0, limit / jnp.sqrt(total + 1e-06))
    own_rows = first_ref.shape[1]
    parts = first_ref.shape[0]
    half, tenth = 0.5 * factor, 0.1 * factor * factor
    basis = basis_ref[...]
    high = basis.astype(BF)
    rest = (basis - high.astype(F32)).astype(BF)
    mine = pl.ds(pl.multiple_of(member * own_rows, own_rows), own_rows)
    copies = []

    def start(source, target):
        copies.append(pltpu.make_async_copy(source, target, sems.at[len(copies)]))
        copies[-1].start()

    low = full[:, mine, :]
    new_first_ref[...] = 0.5 * first_ref[...] + half * low
    new_second_ref[...] = 0.9 * second_ref[...] + tenth * low * low
    start(new_first_ref, out_hbms[0])
    start(new_second_ref, out_hbms[1])
    for i in range(parts):
        for dc in range(2):
            for dx in range(2):
                column = ((side ^ dx) * 2 + (core ^ dc)) * unit
                columns = pl.ds(pl.multiple_of(column, unit), unit)
                lanes = slice(i * unit, (i + 1) * unit)
                ref = core_moms.at[dx] if dc else moms[dx]
                for n, dr in ((n, dr) for n in range(chips) for dr in range(2)):
                    row = ((chip ^ mirrored(n, chips)) * 2 + (core ^ dc ^ dr)) * own_rows
                    rows = pl.ds(pl.multiple_of(row, own_rows), own_rows)
                    low = full[i, rows, columns]
                    first = 0.5 * ref[n, dr, :own_rows, lanes].astype(F32) + half * low
                    second = 0.9 * ref[n, dr, own_rows:, lanes].astype(F32) + tenth * low * low
                    root = second * lax.rsqrt(second) + 1e-08
                    stepped[rows, columns] = first * pl.reciprocal(root, approx=True)
        step = stepped[...].astype(BF)
        products[i] = dot(high, step) + dot(rest, step)
        start(products.at[i], out_hbms[2].at[i])
    for copy in copies:
        copy.wait()


def local(sizes, tokens, cotangent, w_gate, w_up, w_down, basis, first_moment, second_moment):
    groups, members = sizes
    chips = members // 2
    toks, width = tokens.shape
    depth, hidden_size = w_gate.shape
    rank = basis.shape[1]
    unit, half = hidden_size // 4, rank // 2
    own_rows = first_moment.shape[1]
    limit = math.sqrt(first_moment.shape[0] * rank * hidden_size)

    def by_member(value, bits):
        return lax.ppermute(value, "member", [(i, i ^ bits) for i in range(members)])

    def by_group(value, bits):
        return lax.ppermute(value, "group", [(i, i ^ bits) for i in range(groups)])

    def by_chip(value, bits):
        pairs = []
        for g in range(groups):
            for i in range(members):
                j = i ^ bits ^ ((g // 2) % 2)
                pairs.append((g * members + i, g * members + j))
        return lax.ppermute(value, ("group", "member"), pairs)

    parts = first_moment.shape[0]
    block = half + 3 * unit
    own, sent, to_core, mom_mine, both = call(
        functools.partial(pack_kernel, parts),
        [((depth, block), BF)] * 2
        + [((depth + 2 * own_rows, block), BF), ((2 * own_rows, parts * unit), BF), ((2 * toks, width), BF)],
        [
            pltpu.VMEM(basis.shape, F32),
            pltpu.VMEM(first_moment.shape, F32),
            pltpu.VMEM(second_moment.shape, F32),
            pltpu.SemaphoreType.DMA((14,)),
        ],
        0,
        w_down,
        w_gate,
        w_up,
        basis,
        first_moment,
        second_moment,
        tokens,
        cotangent,
        pinned=True,
        mib=16,
    )
    direct = [k for k in range(1, chips) if k & (k - 1) == 0]
    passed = [k for k in range(1, chips) if k & (k - 1)]
    ordered = lax.optimization_barrier

    both_x = by_group(both, 1)
    near = {k: by_chip(sent, 2 * k) for k in reversed(direct)}
    from_core = by_member(to_core, 1)
    groups_of = [direct[:1], direct[1:], passed]

    def forward(which):
        return by_group(jnp.concatenate([near[k] for k in groups_of[which]]), 2)

    for k in passed:
        near[k] = by_member(near[k & (k - 1)], 2 * (k & -k))
    far = [forward(0), forward(1)]
    far[0], from_core = ordered((far[0], from_core))
    moms = jnp.stack([mom_mine, from_core[depth:, : parts * unit]])[None]
    for bit in reversed(direct[1:]):
        moms = jnp.concatenate([moms, by_member(moms, 2 * bit)])
    near, far, both_x, both, moms = ordered((near, far, both_x, both, moms))

    far.append(forward(2))
    both_c = by_member(both, 1)
    both_xc = by_member(both_x, 1)
    moms = jnp.concatenate([moms, by_member(moms, 2)])
    far, both_c, both_xc = ordered((far, both_c, both_xc))

    layout = [(0, 0), (1, 0)]
    for k in range(1, chips):
        i = [k in group for group in groups_of].index(True)
        layout += [(1 + k, 0), (1 + chips + i, groups_of[i].index(k) * depth)]
    four = 4 * toks
    proj, dgu, hidden, full = call(
        functools.partial(first_kernel, members, tuple(layout), depth, half),
        [
            ((four, 2 * half), BF),
            ((four, 2 * unit), BF),
            ((four, unit), BF),
            ((width, block), BF),
        ],
        [],
        2 * four * width * (2 * half + 3 * unit),
        *(both, both_c, both_x, both_xc),
        *(own, from_core, *(near[k] for k in range(1, chips)), *far),
    )
    dgu, moms = ordered((dgu, moms))
    proj_core = by_member(proj, 1)
    moms_x = by_group(moms, 1)
    keep_0, keep_1, send_0, send_1 = call(
        grad_kernel,
        [((toks, width), F32)] * 2 + [((toks, width), BF)] * 2,
        [],
        2 * four * width * 2 * unit,
        dgu,
        full,
    )
    proj_core, send_1 = ordered((proj_core, send_1))
    near_part = by_member(send_1, 1)
    height = rank // chips
    piece = (parts, height, unit)
    lows = call(
        second_kernel,
        [(piece, BF if k else F32) for k in range(chips)],
        [pltpu.VMEM((parts, rank, unit), F32)],
        2 * four * 3 * rank * unit,
        proj,
        proj_core,
        dgu,
        hidden,
    )
    near_part = (keep_1 + near_part.astype(F32)).astype(BF)
    lows, near_part = ordered((lows, near_part))
    arrived = [by_member(lows[k], 2 * k) for k in reversed(range(1, chips))]
    arrived = ordered(arrived)
    grad_side = by_group(near_part, 1)
    share = lows[0]
    for low in arrived:
        share = share + low.astype(F32)
    bit = 2
    while bit < groups:
        sent = share.astype(BF)
        came = by_group(sent, bit)
        moms_x, came = ordered((moms_x, came))
        share = sent.astype(F32) + came.astype(F32)
        bit *= 2
    share = share.astype(BF)

    core_moms = by_member(jnp.stack([moms, moms_x]), 1)
    low_mine = [by_member(share, 2 * k) for k in reversed(range(1, chips))]
    grad_side, low_mine = ordered((grad_side, low_mine))
    low_mine = jnp.stack([share] + low_mine[::-1])
    low_side = by_group(low_mine, 1)
    mine_part = keep_0 + by_member(send_0, 1).astype(F32)
    input_grad = (mine_part + grad_side.astype(F32)).astype(BF)
    low_core = [by_member(low_mine, 1), by_member(low_side, 1)]
    new_first, new_second, updates = call(
        functools.partial(last_kernel, chips, limit),
        [(first_moment.shape, F32), (second_moment.shape, F32), ((parts, depth, hidden_size), F32)],
        [
            pltpu.VMEM((parts, rank, hidden_size), F32),
            pltpu.VMEM((rank, hidden_size), F32),
            pltpu.VMEM(first_moment.shape, F32),
            pltpu.VMEM(second_moment.shape, F32),
            pltpu.VMEM((parts, depth, hidden_size), F32),
            pltpu.SemaphoreType.DMA((parts + 2,)),
        ],
        4 * 3 * depth * rank * hidden_size,
        low_mine,
        low_side,
        *low_core,
        moms,
        moms_x,
        core_moms,
        basis,
        first_moment,
        second_moment,
        results=pltpu.HBM,
    )
    return (input_grad, new_first, new_second, updates)


def solution(mesh):
    sizes = (mesh.shape["group"], mesh.shape["member"])
    tokens = P(("group", "member"), None)
    rows = P("member", None)
    low = P(None, "member", None)
    return jax.shard_map(
        functools.partial(local, sizes),
        mesh=mesh,
        in_specs=(tokens, tokens, rows, rows, rows, rows, low, low),
        out_specs=(tokens, low, low, low),
        check_vma=False,
    )
```
